128 devices in a mesh: shot: 16 (over x_hi, y, core), tile: 8 (over z, x_lo).
Axes of the slice: x: 4 (x_hi: 2, x_lo: 2; x = x_hi * 2 + x_lo), y: 4, z: 4, core: 2. Of those that a mesh axis runs over, the one named last changes fastest.
Arguments:
- courant: float32 [256, 256, 128], P('shot', 'tile'), may hold values from 0.03 to 0.18
- damping: float32 [256, 256, 128], P('shot', 'tile'), may hold values from 0.02 to 0.3
- aperture_block: int32 [16], replicated, may hold values from 0 to 10
- source_cell: int32 [16], P('shot'), may hold values from 0 to 3145727
- receiver_depth: int32 [16], P('shot'), may hold values from 0 to 127
- wavelet: float32 [16, 8], P('shot'), may hold values from -48 to 48
- receiver_data: float32 [16, 8, 96, 256], P('shot', None, None, 'tile'), may hold values from -6 to 6
- forward_state: float32 [16, 2, 96, 256, 128], P('shot', None, None, 'tile'), may hold values from -6 to 6
- adjoint_state: float32 [16, 2, 96, 256, 128], P('shot', None, None, 'tile'), may hold values from -6 to 6
Outputs:
- image: float32 [256, 256, 128], P('shot', 'tile')
The draws below stay inside these ranges and needn't reach their ends.
Inputs may be any that keep to these rules, and one draw needn't show every extreme that they name: Shot s's aperture covers model indices 16 * aperture_block[s] to 16 * aperture_block[s] + 95 of dimension 0. `source_cell`: decodes as x * 96 * 128 + y * 128 + z in aperture coordinates.
All inputs are finite; a program needn't handle non-finite values.
Results may differ from the reference program's by a relative error of at most 0.0003.
Values sent between devices are 32-bit elements; how exact they have to be, the bound alone decides.
A program may use at most 128 MiB of HBM per device.

```python
import math
import jax
import jax.numpy as jnp
import numpy as np
from jax import lax

AY = 96
BY = 16
NZ = 128
STEPS = 8
AX = 256
MY = 256
SHOTS = 16


def set_ends(values, own_key, low, top_value):
    extent = values.shape
    spot = [jax.random.randint(jax.random.fold_in(own_key, axis), (), 0, extent[axis]) for axis in range(len(extent))]
    values = values.at[tuple(spot)].set(low)
    longest = extent.index(max(extent))
    spot[longest] = (spot[longest] + 1) % extent[longest]
    return values.at[tuple(spot)].set(top_value)


def block_scale(rng, extent, pieces, least, high):
    def one(position, parts):
        draws = jax.random.uniform(jax.random.fold_in(jax.random.fold_in(rng, 6), position), (parts,), jnp.float32, least / len(pieces), high / len(pieces))
        return jnp.repeat(jnp.exp(draws), extent[position] // parts).reshape((-1,) + (1,) * (len(extent) - position - 1))

    level = one(*pieces[0])
    for cut in pieces[1:]:
        level = level * one(*cut)
    return level


def rank_table(amount, skew):
    weights = [(1 << 20) // math.isqrt(standing ** skew) + 1 for standing in range(1, amount + 1)]
    width = 1 + sum(weights) // (1 << 30)
    return np.cumsum(np.array([max(1, weight // width) for weight in weights]))


def skewed_ids(key, shape, number_of, lean):
    grid = rank_table(number_of, lean)
    pick = jax.random.randint(jax.random.fold_in(key, 1), shape, 0, int(grid[number_of - 1]))
    grade = jnp.searchsorted(jnp.asarray(grid, jnp.int32), pick, side="right")
    return jax.random.permutation(jax.random.fold_in(key, 2), number_of)[grade].astype(jnp.int32)


def noise(rng, extent, deviation, most, cuts=(), kind=jnp.bfloat16):
    array = jax.random.normal(rng, extent, jnp.float32) * deviation
    if len(cuts) > 0:
        array = block_scale(rng, extent, cuts, -0.22, 0.18) * array
    return jnp.clip(array, min=-most, max=most).astype(kind)


def setup_inputs(seed: int = 0) -> dict:
    key_list = jax.random.split(jax.random.key(seed), 10)
    courant = jnp.clip(jnp.exp(math.log(0.18) - 1.7917595 * jax.random.uniform(key_list[0], (MY, AX, NZ), jnp.float32) ** block_scale(key_list[0], (MY, AX, NZ), ((0, 16), (1, 8)), -0.2, 0.2)), 0.03, 0.18)
    damping = jnp.clip(jnp.exp(math.log(0.3) - 2.7080503 * jax.random.uniform(key_list[1], (MY, AX, NZ), jnp.float32) ** block_scale(key_list[1], (MY, AX, NZ), ((0, 16), (1, 8)), -0.2, 0.2)), 0.02, 0.3)
    aperture_block = set_ends(skewed_ids(key_list[2], (SHOTS,), MY // BY - AY // BY + 1, 2), jax.random.fold_in(key_list[2], 3), 0, (MY // BY - AY // BY + 1) - 1).astype(jnp.int32)
    source_cell = set_ends(jax.random.randint(key_list[3], (SHOTS,), 0, AX * AY * NZ), jax.random.fold_in(key_list[3], 1), 0, (AX * AY * NZ) - 1).astype(jnp.int32)
    receiver_depth = set_ends(jax.random.randint(key_list[4], (SHOTS,), 0, NZ), jax.random.fold_in(key_list[4], 1), 0, NZ - 1).astype(jnp.int32)
    wavelet = noise(key_list[5], (SHOTS, STEPS), 8.0, 48.0, ((0, 16),), jnp.float32)
    receiver_data = noise(key_list[6], (SHOTS, STEPS, AY, AX), 1.0, 6.0, ((0, 16), (3, 8)), jnp.float32)
    forward_state = noise(key_list[7], (SHOTS, 2, AY, AX, NZ), 1.0, 6.0, ((0, 16), (3, 8)), jnp.float32)
    adjoint_state = noise(key_list[8], (SHOTS, 2, AY, AX, NZ), 1.0, 6.0, ((0, 16), (3, 8)), jnp.float32)
    return {"courant": courant, "damping": damping, "aperture_block": aperture_block, "source_cell": source_cell, "receiver_depth": receiver_depth, "wavelet": wavelet, "receiver_data": receiver_data, "forward_state": forward_state, "adjoint_state": adjoint_state}


STENCIL_WEIGHTS = (-205.0 / 72.0, 8.0 / 5.0, -1.0 / 5.0, 8.0 / 315.0, -1.0 / 560.0)


def laplace(field):
    padded = jnp.pad(field, 4)
    first, second, third = field.shape
    total = 3.0 * STENCIL_WEIGHTS[0] * field
    for offset in range(1, 5):
        near = padded[4 + offset:4 + offset + first, 4:4 + second, 4:4 + third] + padded[4 - offset:4 - offset + first, 4:4 + second, 4:4 + third]
        near = near + padded[4:4 + first, 4 + offset:4 + offset + second, 4:4 + third] + padded[4:4 + first, 4 - offset:4 - offset + second, 4:4 + third]
        near = near + padded[4:4 + first, 4:4 + second, 4 + offset:4 + offset + third] + padded[4:4 + first, 4:4 + second, 4 - offset:4 - offset + third]
        total = total + STENCIL_WEIGHTS[offset] * near
    return total


def advance(current, previous, speed, absorb, forcing):
    return (2.0 * current - (1.0 - absorb) * previous + speed * laplace(current) + forcing) / (1.0 + absorb)


def reference(courant, damping, aperture_block, source_cell, receiver_depth, wavelet, receiver_data, forward_state, adjoint_state):
    index_y = jnp.arange(AY, dtype=jnp.int32).reshape(-1, 1, 1)
    index_x = jnp.arange(AX, dtype=jnp.int32).reshape(1, -1, 1)
    index_z = jnp.arange(NZ, dtype=jnp.int32).reshape(1, 1, -1)

    def one_shot(image, inputs):
        block, cell, depth, amplitudes, records, fstate, astate = inputs
        first_row = (block * BY).astype(jnp.int32)
        speed = lax.dynamic_slice_in_dim(courant, first_row, AY, 0)
        absorb = lax.dynamic_slice_in_dim(damping, first_row, AY, 0)
        source_x = cell // (AY * NZ)
        source_y = (cell // NZ) % AY
        source_z = cell % NZ
        source = ((index_y == source_y) & (index_x == source_x) & (index_z == source_z)).astype(jnp.float32)
        plane = (index_z == depth).astype(jnp.float32)

        def forward(carry, amplitude):
            current, previous = carry
            updated = advance(current, previous, speed, absorb, amplitude * source)
            return (updated, current), updated

        _, snapshots = lax.scan(forward, (fstate[0], fstate[1]), amplitudes)

        def backward(carry, inputs_step):
            current, previous, summed = carry
            snapshot, record = inputs_step
            updated = advance(current, previous, speed, absorb, record[:, :, None] * plane)
            return (updated, current, summed + snapshot * updated), None

        start = (astate[0], astate[1], jnp.zeros((AY, AX, NZ), jnp.float32))
        (_, _, summed), _ = lax.scan(backward, start, (snapshots[::-1], records[::-1]))
        partial_value = summed / STEPS
        region = lax.dynamic_slice_in_dim(image, first_row, AY, 0) + partial_value
        return lax.dynamic_update_slice_in_dim(image, region, first_row, 0), None

    image = jnp.zeros((MY, AX, NZ), jnp.float32)
    inputs = (aperture_block, source_cell, receiver_depth, wavelet, receiver_data, forward_state, adjoint_state)
    image, _ = lax.scan(one_shot, image, inputs)
    return image
```

```python
import functools
import jax
import jax.numpy as jnp
import numpy as np
from jax import lax
from jax.experimental import pallas as pl
from jax.experimental.pallas import tpu as pltpu
from jax.sharding import PartitionSpec as P

MESH_ID = pl.DeviceIdType.MESH
SCALE = 5040.0
WEIGHTS = (-43050.0, 8064.0, -1008.0, 128.0, -9.0)
CENTRES = (-43008.0, -42.0)
NY, NX, NZ = 96, 32, 128
PY = 104
PX = 104


def band_matrix(size, centre):
    band = centre * np.eye(size, dtype=np.float32)
    for offset in range(1, 5):
        band += WEIGHTS[offset] * (np.eye(size, k=offset) + np.eye(size, k=-offset))
    return band


def band_pair():
    deep, wide = band_matrix(NZ, CENTRES[0]), band_matrix(NY, CENTRES[1])
    return (jnp.asarray(np.concatenate([deep, deep], axis=0), jnp.bfloat16),
            jnp.asarray(np.concatenate([wide, wide], axis=1), jnp.bfloat16))


def step_kernel(fwd, adj, extra, speed, absorb, band_z, band_y, out, F, Z, A, C, E, T, image, ssem, rsem):
    s = lax.axis_index("shot")
    t = lax.axis_index("tile")
    core = s % 2
    place = 2 * (t // 2) + core
    left = (s + 1 - 2 * core, t - 2 * (1 - core))
    right = (s + 1 - 2 * core, t + 2 * core)
    has_left = place > 0
    has_right = place < 7

    def halo(f, slot, par, side):
        if side == 0:
            return pltpu.make_async_remote_copy(
                src_ref=F.at[f, slot, pl.ds(4, 4), pl.ds(0, NY), :],
                dst_ref=F.at[f, slot, pl.ds(36, 4), pl.ds(0, NY), :],
                send_sem=ssem.at[f, 0, par], recv_sem=rsem.at[f, 0, par],
                device_id=left, device_id_type=MESH_ID)
        return pltpu.make_async_remote_copy(
            src_ref=F.at[f, slot, pl.ds(32, 4), pl.ds(0, NY), :],
            dst_ref=F.at[f, slot, pl.ds(0, 4), pl.ds(0, NY), :],
            send_sem=ssem.at[f, 1, par], recv_sem=rsem.at[f, 1, par],
            device_id=right, device_id_type=MESH_ID)

    def send(f, slot, par, side):
        @pl.when(has_left if side == 0 else has_right)
        def _():
            halo(f, slot, par, side).start()

    def wait(f, slot, par):
        @pl.when(has_left)
        def _():
            halo(f, slot, par, 0).wait_send()
            halo(f, slot, par, 1).wait_recv()

        @pl.when(has_right)
        def _():
            halo(f, slot, par, 1).wait_send()
            halo(f, slot, par, 0).wait_recv()

    barrier = pltpu.get_barrier_semaphore()

    @pl.when(has_left)
    def _():
        pl.semaphore_signal(barrier, inc=1, device_id=left, device_id_type=MESH_ID)

    @pl.when(has_right)
    def _():
        pl.semaphore_signal(barrier, inc=1, device_id=right, device_id_type=MESH_ID)

    zero_side = jnp.zeros((4, NY, NZ), jnp.float32)
    for f in range(2):
        def clear(slot, carry):
            @pl.when(place == 0)
            def _():
                F[f, slot, pl.ds(0, 4), pl.ds(0, NY), :] = zero_side

            @pl.when(place == 7)
            def _():
                F[f, slot, pl.ds(36, 4), pl.ds(0, NY), :] = zero_side
            return carry
        lax.fori_loop(0, 6, clear, 0)

    def load_states(j, carry):
        rows = pl.ds(pl.multiple_of(8 * j, 8), 8)
        for x in range(NX):
            picked = pl.ds(8 * NX * j + x, 8, stride=NX)
            for f, source in ((0, fwd), (1, adj)):
                F[f, 1, 4 + x, rows, :] = source[0, picked, :]
                F[f, 0, 4 + x, rows, :] = source[1, picked, :]
        return carry

    lax.fori_loop(0, NY // 8, load_states, 0)

    pl.semaphore_wait(barrier, has_left.astype(jnp.int32) + has_right.astype(jnp.int32))

    for f in range(2):
        send(f, 1, 0, 0)
        send(f, 1, 0, 1)

    lane = lax.broadcasted_iota(jnp.int32, (8, NZ), 1)
    row = lax.broadcasted_iota(jnp.int32, (8, NZ), 0)
    depth = jnp.broadcast_to(extra[0, pl.ds(0, 8), pl.ds(34, 1)], (8, NZ))
    plane = jnp.where(lane.astype(jnp.float32) == depth, 0.5, 0.0)
    cell = jnp.broadcast_to(extra[0, pl.ds(0, 8), pl.ds(33, 1)], (8, NZ))

    turns = [(depth + m) - jnp.where(depth + m >= NZ, float(NZ), 0.0) for m in range(8)]

    def load_model(j, carry):
        rows = pl.ds(pl.multiple_of(8 * j, 8), 8)
        for x in range(NX):
            picked = pl.ds(8 * NX * j + x, 8, stride=NX)
            placed = jnp.zeros((8, NZ), jnp.float32)
            for m in range(8):
                value = jnp.broadcast_to(extra[m, rows, pl.ds(x, 1)], (8, NZ))
                placed = jnp.where(lane.astype(jnp.float32) == turns[m], value, placed)
            T[x, rows, :] = placed
            A[x, rows, :] = 2.0 / (1.0 + absorb[picked, :])
            C[x, rows, :] = speed[picked, :] * (0.5 / SCALE)
            index = (place * NX + x) * (NY * NZ) + (row + 8 * j) * NZ + lane
            E[x, rows, :] = jnp.where(index.astype(jnp.float32) == cell, 0.5, 0.0)
            image[x, rows, :] = jnp.zeros((8, NZ), jnp.float32)
        return carry

    lax.fori_loop(0, NY // 8, load_model, 0)

    def across(f, slot, x):
        u = F[f, slot, pl.ds(4 + x, 2), pl.ds(0, NY), :]
        high = u.astype(jnp.bfloat16)
        low = (u - high.astype(jnp.float32)).astype(jnp.bfloat16)
        rows = jnp.concatenate([high.reshape(2 * NY, NZ), low.reshape(2 * NY, NZ)], axis=1)
        deep = jnp.dot(rows, band_z[...], preferred_element_type=jnp.float32)
        sides = jnp.concatenate([jnp.concatenate([high[0], high[1]], axis=1),
                                 jnp.concatenate([low[0], low[1]], axis=1)], axis=0)
        wide = jnp.dot(band_y[...], sides, preferred_element_type=jnp.float32)
        Z[f, x, pl.ds(0, NY), :] = deep[:NY] + wide[:, :NZ]
        Z[f, x + 1, pl.ds(0, NY), :] = deep[NY:] + wide[:, NZ:]

    def advance(f, cur, prev, new, other, n):
        wait(f, cur, (n - 1) % 2)
        amp = jnp.broadcast_to(extra[n - 1, pl.ds(0, 8), pl.ds(32, 1)], (8, NZ))

        def planes(i, carry):
            x = 2 * i
            across(1 - f, cur if f == 0 else new, x)
            for j in range(NY // 8):
                crow = pl.ds(8 * j, 8)
                rows = crow
                wide = F[f, cur, pl.ds(x, 10), rows, :]
                u = wide[4:6]
                acc = Z[f, pl.ds(x, 2), crow, :]
                for k in range(1, 5):
                    acc = acc + WEIGHTS[k] * (wide[4 + k:6 + k] + wide[4 - k:6 - k])
                v = F[f, prev, pl.ds(4 + x, 2), rows, :]
                if f == 0:
                    force = E[pl.ds(x, 2), crow, :] * amp[None]
                else:
                    force = jnp.stack([pltpu.roll(T[x + h, crow, :], NZ - (8 - n), 1) * plane for h in range(2)])
                w = v + A[pl.ds(x, 2), crow, :] * ((u - v) + (C[pl.ds(x, 2), crow, :] * acc + force))
                F[f, new, pl.ds(4 + x, 2), rows, :] = w
                if other is not None:
                    image[pl.ds(x, 2), crow, :] += w * F[1 - f, other, pl.ds(4 + x, 2), rows, :]
            return carry

        for first, last, side in ((0, 2, 0), (14, 16, 1), (2, 14, None)):
            lax.fori_loop(first, last, planes, 0)
            if side is not None:
                @pl.when(n < 8)
                def _():
                    send(f, new, n % 2, side)

    def first_across(i, carry):
        across(0, 1, 2 * i)
        return carry

    lax.fori_loop(0, NX // 2, first_across, 0)

    def early(n, carry):
        for f in range(2):
            advance(f, n, n - 1, n + 1, None, n)
        return carry

    lax.fori_loop(1, 5, early, 0)

    def late(n, carry):
        for f in range(2):
            advance(f, n % 2 + 4 * (5 // n), (n - 1) % 2 + 4 * (6 // n), (n + 1) % 2, 10 - n, n)
        return carry

    lax.fori_loop(5, 9, late, 0)

    def store(j, carry):
        rows = pl.ds(pl.multiple_of(8 * j, 8), 8)
        for x in range(NX):
            out[pl.ds(8 * NX * j + x, 8, stride=NX), :] = image[x, rows, :] * 0.125
        return carry

    lax.fori_loop(0, NY // 8, store, 0)


def run_steps(fwd, adj, extra, speed, absorb):
    vm = pl.BlockSpec(memory_space=pltpu.VMEM)
    return pl.pallas_call(
        step_kernel,
        out_shape=jax.ShapeDtypeStruct((NY * NX, NZ), jnp.float32),
        in_specs=[vm] * 7,
        out_specs=vm,
        scratch_shapes=[
            pltpu.VMEM((2, 6, NX + 8, PY, NZ), jnp.float32),
            pltpu.VMEM((2, NX, PX, NZ), jnp.float32),
            pltpu.VMEM((NX, PX, NZ), jnp.float32),
            pltpu.VMEM((NX, PX, NZ), jnp.float32),
            pltpu.VMEM((NX, PX, NZ), jnp.float32),
            pltpu.VMEM((NX, PX, NZ), jnp.float32),
            pltpu.VMEM((NX, PX, NZ), jnp.float32),
            pltpu.SemaphoreType.DMA((2, 2, 2)),
            pltpu.SemaphoreType.DMA((2, 2, 2)),
        ],
        compiler_params=pltpu.CompilerParams(collective_id=1, has_side_effects=True, vmem_limit_bytes=62 << 20),
        name="wave_steps",
    )(fwd, adj, extra, speed, absorb, *band_pair())


def swap_pairs():
    pairs = []
    for s in range(16):
        for t in range(8):
            core, low = s % 2, t % 2
            pairs.append((s * 8 + t, (s - core + low) * 8 + (t - low + core)))
    return pairs


def body(courant, damping, aperture_block, source_cell, receiver_depth, wavelet, receiver_data,
         forward_state, adjoint_state):
    member = lax.axis_index("shot")
    first = aperture_block[member]
    axes = ("shot", "tile")
    pairs = swap_pairs()

    def swap(value):
        return lax.ppermute(value, axes, pairs)

    def window(model):
        whole = lax.all_gather(model, "shot", axis=0, tiled=True)
        return lax.dynamic_slice_in_dim(whole, first * 16, NY, 0)

    speed = window(courant).reshape(NY * NX, NZ)
    absorb = window(damping).reshape(NY * NX, NZ)
    records = jnp.pad(receiver_data[0], ((0, 0), (0, 0), (0, NZ - NX)))
    lane = lax.broadcasted_iota(jnp.int32, (8, NY, NZ), 2)
    extra = jnp.where(lane == 32, wavelet[0][:, None, None], records)
    extra = jnp.where(lane == 33, source_cell[0].astype(jnp.float32), extra)
    extra = jnp.where(lane == 34, receiver_depth[0].astype(jnp.float32), extra)
    partial = run_steps(
        swap(forward_state[0].reshape(2, NY * NX, NZ)), swap(adjoint_state[0].reshape(2, NY * NX, NZ)),
        swap(extra), swap(speed), swap(absorb))
    partial = swap(partial).reshape(NY, NX, NZ)
    whole = jnp.zeros((256, NX, NZ), jnp.float32)
    whole = lax.dynamic_update_slice_in_dim(whole, partial, first * 16, 0)
    return lax.psum_scatter(whole, "shot", scatter_dimension=0, tiled=True)


def solution(mesh):
    placed = (
        P("shot", "tile", None),
        P("shot", "tile", None),
        P(),
        P("shot"),
        P("shot"),
        P("shot", None),
        P("shot", None, None, "tile"),
        P("shot", None, None, "tile", None),
        P("shot", None, None, "tile", None),
    )
    return jax.shard_map(
        body, mesh=mesh, in_specs=placed, out_specs=P("shot", "tile", None), check_vma=False
    )
```

```python
import functools
import jax
import jax.numpy as jnp
import numpy as np
from jax import lax
from jax.experimental import pallas as pl
from jax.experimental.pallas import tpu as pltpu
from jax.sharding import PartitionSpec as P

MESH_ID = pl.DeviceIdType.MESH
SCALE = 5040.0
WEIGHTS = (-43050.0, 8064.0, -1008.0, 128.0, -9.0)
CENTRES = (-43008.0, -42.0)
NY, NX, NZ = 96, 32, 128
PY = 104
PX = 104
CHUNK = 128


def band_matrix(size, centre):
    band = centre * np.eye(size, dtype=np.float32)
    for offset in range(1, 5):
        band += WEIGHTS[offset] * (np.eye(size, k=offset) + np.eye(size, k=-offset))
    return band


def band_pair():
    deep, wide = band_matrix(NZ, CENTRES[0]), band_matrix(NY, CENTRES[1])
    return (jnp.asarray(np.concatenate([deep, deep], axis=0), jnp.bfloat16),
            jnp.asarray(np.concatenate([wide, wide], axis=1), jnp.bfloat16))


def step_kernel(fwd, adj, extra, window, band_z, band_y, out, F, Z, A, C, E, T, image, ssem, rsem):
    s = lax.axis_index("shot")
    t = lax.axis_index("tile")
    core = s % 2
    place = 2 * (t // 2) + core
    left = (s + 1 - 2 * core, t - 2 * (1 - core))
    right = (s + 1 - 2 * core, t + 2 * core)
    has_left = place > 0
    has_right = place < 7

    def halo(f, slot, par, side):
        if side == 0:
            return pltpu.make_async_remote_copy(
                src_ref=F.at[f, slot, pl.ds(4, 4), pl.ds(0, NY), :],
                dst_ref=F.at[f, slot, pl.ds(36, 4), pl.ds(0, NY), :],
                send_sem=ssem.at[f, 0, par], recv_sem=rsem.at[f, 0, par],
                device_id=left, device_id_type=MESH_ID)
        return pltpu.make_async_remote_copy(
            src_ref=F.at[f, slot, pl.ds(32, 4), pl.ds(0, NY), :],
            dst_ref=F.at[f, slot, pl.ds(0, 4), pl.ds(0, NY), :],
            send_sem=ssem.at[f, 1, par], recv_sem=rsem.at[f, 1, par],
            device_id=right, device_id_type=MESH_ID)

    def send(f, slot, par, side):
        @pl.when(has_left if side == 0 else has_right)
        def _():
            halo(f, slot, par, side).start()

    def wait(f, slot, par):
        @pl.when(has_left)
        def _():
            halo(f, slot, par, 0).wait_send()
            halo(f, slot, par, 1).wait_recv()

        @pl.when(has_right)
        def _():
            halo(f, slot, par, 1).wait_send()
            halo(f, slot, par, 0).wait_recv()

    barrier = pltpu.get_barrier_semaphore()

    @pl.when(has_left)
    def _():
        pl.semaphore_signal(barrier, inc=1, device_id=left, device_id_type=MESH_ID)

    @pl.when(has_right)
    def _():
        pl.semaphore_signal(barrier, inc=1, device_id=right, device_id_type=MESH_ID)

    zero_side = jnp.zeros((4, NY, NZ), jnp.float32)
    for f in range(2):
        def clear(slot, carry):
            @pl.when(place == 0)
            def _():
                F[f, slot, pl.ds(0, 4), pl.ds(0, NY), :] = zero_side

            @pl.when(place == 7)
            def _():
                F[f, slot, pl.ds(36, 4), pl.ds(0, NY), :] = zero_side
            return carry
        lax.fori_loop(0, 6, clear, 0)

    def load_states(j, carry):
        rows = pl.ds(pl.multiple_of(8 * j, 8), 8)
        for x in range(NX):
            picked = pl.ds(8 * NX * j + x, 8, stride=NX)
            for f, source in ((0, fwd), (1, adj)):
                F[f, 1, 4 + x, rows, :] = source[0, picked, :]
                F[f, 0, 4 + x, rows, :] = source[1, picked, :]
        return carry

    lax.fori_loop(0, NY // 8, load_states, 0)

    pl.semaphore_wait(barrier, has_left.astype(jnp.int32) + has_right.astype(jnp.int32))

    for f in range(2):
        send(f, 1, 0, 0)
        send(f, 1, 0, 1)

    lane = lax.broadcasted_iota(jnp.int32, (8, NZ), 1)
    row = lax.broadcasted_iota(jnp.int32, (8, NZ), 0)
    depth = jnp.broadcast_to(extra[0, pl.ds(0, 8), pl.ds(34, 1)], (8, NZ))
    plane = jnp.where(lane.astype(jnp.float32) == depth, 0.5, 0.0)
    cell = jnp.broadcast_to(extra[0, pl.ds(0, 8), pl.ds(33, 1)], (8, NZ))

    turns = [(depth + m) - jnp.where(depth + m >= NZ, float(NZ), 0.0) for m in range(8)]

    def load_model(j, carry):
        rows = pl.ds(pl.multiple_of(8 * j, 8), 8)
        for x in range(NX):
            picked = pl.ds(8 * NX * j + x, 8, stride=NX)
            placed = jnp.zeros((8, NZ), jnp.float32)
            for m in range(8):
                value = jnp.broadcast_to(extra[m, rows, pl.ds(x, 1)], (8, NZ))
                placed = jnp.where(lane.astype(jnp.float32) == turns[m], value, placed)
            T[x, rows, :] = placed
            A[x, rows, :] = 2.0 / (1.0 + window[1, picked, :])
            C[x, rows, :] = window[0, picked, :] * (0.5 / SCALE)
            index = (place * NX + x) * (NY * NZ) + (row + 8 * j) * NZ + lane
            E[x, rows, :] = jnp.where(index.astype(jnp.float32) == cell, 0.5, 0.0)
            image[x, rows, :] = jnp.zeros((8, NZ), jnp.float32)
        return carry

    lax.fori_loop(0, NY // 8, load_model, 0)

    def across(f, slot, x):
        u = F[f, slot, pl.ds(4 + x, 2), pl.ds(0, NY), :]
        high = u.astype(jnp.bfloat16)
        low = (u - high.astype(jnp.float32)).astype(jnp.bfloat16)
        rows = jnp.concatenate([high.reshape(2 * NY, NZ), low.reshape(2 * NY, NZ)], axis=1)
        deep = jnp.dot(rows, band_z[...], preferred_element_type=jnp.float32)
        sides = jnp.concatenate([jnp.concatenate([high[0], high[1]], axis=1),
                                 jnp.concatenate([low[0], low[1]], axis=1)], axis=0)
        wide = jnp.dot(band_y[...], sides, preferred_element_type=jnp.float32)
        Z[f, x, pl.ds(0, NY), :] = deep[:NY] + wide[:, :NZ]
        Z[f, x + 1, pl.ds(0, NY), :] = deep[NY:] + wide[:, NZ:]

    def advance(f, cur, prev, new, other, n):
        wait(f, cur, (n - 1) % 2)
        amp = jnp.broadcast_to(extra[n - 1, pl.ds(0, 8), pl.ds(32, 1)], (8, NZ))

        def planes(i, carry):
            x = 2 * i
            across(1 - f, cur if f == 0 else new, x)
            for j in range(NY // 8):
                crow = pl.ds(8 * j, 8)
                rows = crow
                wide = F[f, cur, pl.ds(x, 10), rows, :]
                u = wide[4:6]
                acc = Z[f, pl.ds(x, 2), crow, :]
                for k in range(1, 5):
                    acc = acc + WEIGHTS[k] * (wide[4 + k:6 + k] + wide[4 - k:6 - k])
                v = F[f, prev, pl.ds(4 + x, 2), rows, :]
                if f == 0:
                    force = E[pl.ds(x, 2), crow, :] * amp[None]
                else:
                    force = jnp.stack([pltpu.roll(T[x + h, crow, :], NZ - (8 - n), 1) * plane for h in range(2)])
                w = v + A[pl.ds(x, 2), crow, :] * ((u - v) + (C[pl.ds(x, 2), crow, :] * acc + force))
                F[f, new, pl.ds(4 + x, 2), rows, :] = w
                if other is not None:
                    image[pl.ds(x, 2), crow, :] += w * F[1 - f, other, pl.ds(4 + x, 2), rows, :]
            return carry

        for first, last, side in ((0, 2, 0), (14, 16, 1), (2, 14, None)):
            lax.fori_loop(first, last, planes, 0)
            if side is not None:
                @pl.when(n < 8)
                def _():
                    send(f, new, n % 2, side)

    def first_across(i, carry):
        across(0, 1, 2 * i)
        return carry

    lax.fori_loop(0, NX // 2, first_across, 0)

    def early(n, carry):
        for f in range(2):
            advance(f, n, n - 1, n + 1, None, n)
        return carry

    lax.fori_loop(1, 5, early, 0)

    def late(n, carry):
        for f in range(2):
            advance(f, n % 2 + 4 * (5 // n), (n - 1) % 2 + 4 * (6 // n), (n + 1) % 2, 10 - n, n)
        return carry

    lax.fori_loop(5, 9, late, 0)

    def store(j, carry):
        rows = pl.ds(pl.multiple_of(8 * j, 8), 8)
        for x in range(NX):
            out[pl.ds(8 * NX * j + x, 8, stride=NX), :] = image[x, rows, :] * 0.125
        return carry

    lax.fori_loop(0, NY // 8, store, 0)


def run_steps(fwd, adj, extra, window):
    vm = pl.BlockSpec(memory_space=pltpu.VMEM)
    return pl.pallas_call(
        step_kernel,
        out_shape=jax.ShapeDtypeStruct((NY * NX, NZ), jnp.float32),
        in_specs=[vm] * 6,
        out_specs=vm,
        scratch_shapes=[
            pltpu.VMEM((2, 6, NX + 8, PY, NZ), jnp.float32),
            pltpu.VMEM((2, NX, PX, NZ), jnp.float32),
            pltpu.VMEM((NX, PX, NZ), jnp.float32),
            pltpu.VMEM((NX, PX, NZ), jnp.float32),
            pltpu.VMEM((NX, PX, NZ), jnp.float32),
            pltpu.VMEM((NX, PX, NZ), jnp.float32),
            pltpu.VMEM((NX, PX, NZ), jnp.float32),
            pltpu.SemaphoreType.DMA((2, 2, 2)),
            pltpu.SemaphoreType.DMA((2, 2, 2)),
        ],
        compiler_params=pltpu.CompilerParams(collective_id=1, has_side_effects=True, vmem_limit_bytes=62 << 20),
        name="wave_steps",
    )(fwd, adj, extra, window, *band_pair())


def position():
    s = lax.axis_index("shot")
    t = lax.axis_index("tile")
    return s // 8, (s // 2) % 4, s % 2, t // 2, t % 2


def device(xh, y, core, z, xl):
    return (xh * 8 + y * 2 + core, z * 2 + xl)


def meet(xh, y, core, z, xl):
    barrier = pltpu.get_barrier_semaphore()
    peers = []
    for a in range(2):
        for b in range(2):
            for e in range(2):
                if a or b or e:
                    peers.append(device((xh + a) % 2, y, (core + b) % 2, z, (xl + e) % 2))
    for d in range(1, 4):
        peers.append(device(xh, (y + d) % 4, core, z, xl))
    for peer in peers:
        pl.semaphore_signal(barrier, inc=1, device_id=peer, device_id_type=MESH_ID)
    pl.semaphore_wait(barrier, len(peers))


def gather_kernel(blocks, model, fwd, adj, extra, fwd_out, adj_out, extra_out, window,
                  line, packed, ring, xsend, xrecv, fsend, ysend, yrecv, ssend, srecv, local):
    xh, y, core, z, xl = position()
    meet(xh, y, core, z, xl)
    away = core != xl
    home = core == xl

    def remote(source, target, send, recv, peer):
        return pltpu.make_async_remote_copy(src_ref=source, dst_ref=target, send_sem=send, recv_sem=recv,
                                            device_id=peer, device_id_type=MESH_ID)

    def own(k, peer):
        return remote(model, line.at[xh, core], xsend.at[k], xrecv.at[xh, core], peer)

    cross = own(0, device(1 - xh, y, xl, z, 1 - xl))
    pair = own(1, device(xh, y, xl, z, 1 - xl))
    inside = own(2, device(xh, y, 1 - core, z, xl))
    keep = pltpu.make_async_copy(model, line.at[xh, core], local.at[0])
    pair.start()
    cross.start()
    pl.when(away)(inside.start)
    pl.when(home)(keep.start)

    partner = device(xh, y, xl, z, core)
    moves = []
    for k, (source, target) in enumerate(((fwd, fwd_out), (adj, adj_out), (extra, extra_out))):
        moves.append((remote(source, target, ssend.at[k], srecv.at[k], partner),
                      pltpu.make_async_copy(source, target, local.at[1 + k])))
    for far, near in moves:
        pl.when(away)(far.start)
        pl.when(home)(near.start)

    def arrived(a, b):
        remote(line.at[a, b], line.at[a, b], xsend.at[0], xrecv.at[a, b], partner).wait_recv()

    def forward(b):
        return remote(line.at[xh, b], line.at[xh, b], fsend.at[b], xrecv.at[xh, b],
                      device(1 - xh, y, core, z, 1 - xl))

    @pl.when(away)
    def _():
        for b in range(2):
            arrived(xh, b)
            forward(b).start()

    @pl.when(home)
    def _():
        keep.wait()
        arrived(xh, 1 - core)

    for b in range(2):
        arrived(1 - xh, b)

    def pick(target, d):
        first = blocks[xh * 8 + ((y + d) % 4) * 2 + xl]
        for b in range(2):
            half = (2 * y + b < first).astype(jnp.int32)

            def rows(i, carry):
                part = pl.ds(pl.multiple_of(64 * i, 64), 64)
                target[b, :, part, :] = line[half, b, :, part, :]
                return carry
            lax.fori_loop(0, 8, rows, 0)

    def round_trip(d):
        return remote(packed.at[d - 1], ring.at[d], ysend.at[d - 1], yrecv.at[d - 1],
                      device(xh, (y + d) % 4, core, z, xl))

    for d in (2, 1, 3):
        pick(packed.at[d - 1], d)
        round_trip(d).start()
    pick(ring.at[0], 0)
    for d in (1, 3, 2):
        round_trip(d).wait()

    first = blocks[xh * 8 + y * 2 + xl]
    for k in range(6):
        j = first + k
        place = (y - (j // 2) % 4 + 4) % 4
        parity = j % 2

        def rows(i, carry):
            part = pl.ds(pl.multiple_of(64 * i, 64), 64)
            window[:, pl.ds(pl.multiple_of(512 * k + 64 * i, 64), 64), :] = ring[place, parity, :, part, :]
            return carry
        lax.fori_loop(0, 8, rows, 0)

    pair.wait_send()
    cross.wait_send()

    @pl.when(away)
    def _():
        inside.wait_send()
        for b in range(2):
            forward(b).wait_send()
        for far, near in moves:
            far.wait()

    @pl.when(home)
    def _():
        for far, near in moves:
            near.wait()


def run_gather(blocks, model, fwd, adj, extra):
    vm = pl.BlockSpec(memory_space=pltpu.VMEM)
    anywhere = pl.BlockSpec(memory_space=pl.ANY)
    like = lambda v: jax.ShapeDtypeStruct(v.shape, v.dtype)
    dma = pltpu.SemaphoreType.DMA
    return pl.pallas_call(
        gather_kernel,
        out_shape=[like(fwd), like(adj), like(extra), jax.ShapeDtypeStruct((2, NY * NX, NZ), jnp.float32)],
        in_specs=[pl.BlockSpec(memory_space=pltpu.SMEM)] + [anywhere] * 4,
        out_specs=[anywhere] * 3 + [vm],
        scratch_shapes=[
            pltpu.VMEM((2, 2, 2, 512, NZ), jnp.float32),
            pltpu.VMEM((3, 2, 2, 512, NZ), jnp.float32),
            pltpu.VMEM((4, 2, 2, 512, NZ), jnp.float32),
            dma((3,)), dma((2, 2)), dma((2,)), dma((3,)), dma((3,)), dma((3,)), dma((3,)), dma((4,)),
        ],
        compiler_params=pltpu.CompilerParams(collective_id=2, has_side_effects=True, vmem_limit_bytes=24 << 20),
        name="place",
    )(blocks, model, fwd, adj, extra)


def sum_kernel(blocks, partial, out, packed, ring, totals, line, ysend, yrecv, xsend, xrecv):
    xh, y, core, z, xl = position()
    meet(xh, y, core, z, xl)

    def choose(first, row, b):
        half = (2 * row + b < first).astype(jnp.int32)
        step = 8 * half + 2 * row + b - first
        inside = (step >= 0).astype(jnp.int32) * (step < 6).astype(jnp.int32)
        return half + 2 * (1 - inside), step

    def turn(d, q):
        return pltpu.make_async_remote_copy(
            src_ref=packed.at[q, d - 1], dst_ref=ring.at[q, d], send_sem=ysend.at[q, d - 1], recv_sem=yrecv.at[q, d - 1],
            device_id=device(xh, (y + d) % 4, core, z, xl), device_id_type=MESH_ID)

    def pick(target, d, q):
        first = blocks[xh * 8 + y * 2 + xl]
        for b in range(2):
            half, step = choose(first, (y + d) % 4, b)
            target[b] = partial[jnp.clip(step, 0, 5), pl.ds(CHUNK * q, CHUNK), :]

    for q in range(512 // CHUNK):
        for d in (2, 1, 3):
            pick(packed.at[q, d - 1], d, q)
            turn(d, q).start()
        pick(ring.at[q, 0], 0, q)

    def spread(k, q):
        a, b = k // 2, k % 2
        return pltpu.make_async_remote_copy(
            src_ref=totals.at[q, k], dst_ref=line.at[q, xh * 2 + xl], send_sem=xsend.at[q, k],
            recv_sem=xrecv.at[q, xh * 2 + xl], device_id=device(a, y, b, z, core), device_id_type=MESH_ID)

    def mine(k):
        return (xh == k // 2) & (core == k % 2) & (xl == core)

    for q in range(512 // CHUNK):
        for d in (1, 3, 2):
            turn(d, q).wait_recv()
        for k in range(4):
            a, b = k // 2, k % 2
            total = jnp.zeros((CHUNK, NZ), jnp.float32)
            for d in range(4):
                first = blocks[xh * 8 + ((y - d + 4) % 4) * 2 + xl]
                half, step = choose(first, y, b)
                total = total + jnp.where(jnp.full((CHUNK, NZ), half, jnp.int32) == a, ring[q, d, b], 0.0)
            totals[q, k] = total

            @pl.when(jnp.logical_not(mine(k)))
            def _():
                spread(k, q).start()

            @pl.when(mine(k))
            def _():
                line[q, xh * 2 + xl] = totals[q, k]

    for q in range(512 // CHUNK):
        for k in range(4):
            source = device(k // 2, y, xl, z, k % 2)

            @pl.when(jnp.logical_not((xh * 2 + xl == k) & (xl == core)))
            def _():
                pltpu.make_async_remote_copy(
                    src_ref=line.at[q, k], dst_ref=line.at[q, k], send_sem=xsend.at[q, k], recv_sem=xrecv.at[q, k],
                    device_id=source, device_id_type=MESH_ID).wait_recv()
        out[pl.ds(CHUNK * q, CHUNK), :] = (line[q, 0] + line[q, 1]) + (line[q, 2] + line[q, 3])

    for q in range(512 // CHUNK):
        for d in (1, 3, 2):
            turn(d, q).wait_send()
        for k in range(4):
            @pl.when(jnp.logical_not(mine(k)))
            def _():
                spread(k, q).wait_send()


def run_sum(blocks, partial):
    vm = pl.BlockSpec(memory_space=pltpu.VMEM)
    dma = pltpu.SemaphoreType.DMA
    count = 512 // CHUNK
    return pl.pallas_call(
        sum_kernel,
        out_shape=jax.ShapeDtypeStruct((512, NZ), jnp.float32),
        in_specs=[pl.BlockSpec(memory_space=pltpu.SMEM), vm],
        out_specs=vm,
        scratch_shapes=[
            pltpu.VMEM((count, 3, 2, CHUNK, NZ), jnp.float32),
            pltpu.VMEM((count, 4, 2, CHUNK, NZ), jnp.float32),
            pltpu.VMEM((count, 4, CHUNK, NZ), jnp.float32),
            pltpu.VMEM((count, 4, CHUNK, NZ), jnp.float32),
            dma((count, 3)), dma((count, 3)), dma((count, 4)), dma((count, 4)),
        ],
        compiler_params=pltpu.CompilerParams(collective_id=3, has_side_effects=True, vmem_limit_bytes=24 << 20),
        name="image_sum",
    )(blocks, partial)


def body(courant, damping, aperture_block, source_cell, receiver_depth, wavelet, receiver_data,
         forward_state, adjoint_state):
    records = jnp.pad(receiver_data[0], ((0, 0), (0, 0), (0, NZ - NX)))
    lane = lax.broadcasted_iota(jnp.int32, (8, NY, NZ), 2)
    extra = jnp.where(lane == 32, wavelet[0][:, None, None], records)
    extra = jnp.where(lane == 33, source_cell[0].astype(jnp.float32), extra)
    extra = jnp.where(lane == 34, receiver_depth[0].astype(jnp.float32), extra)
    model = jnp.stack([courant.reshape(512, NZ), damping.reshape(512, NZ)])
    fwd, adj, extra, window = run_gather(
        aperture_block, model, forward_state[0].reshape(2, NY * NX, NZ), adjoint_state[0].reshape(2, NY * NX, NZ), extra)
    partial = run_steps(fwd, adj, extra, window).reshape(6, 512, NZ)
    return run_sum(aperture_block, partial).reshape(16, NX, NZ)


def solution(mesh):
    placed = (
        P("shot", "tile", None),
        P("shot", "tile", None),
        P(),
        P("shot"),
        P("shot"),
        P("shot", None),
        P("shot", None, None, "tile"),
        P("shot", None, None, "tile", None),
        P("shot", None, None, "tile", None),
    )
    return jax.shard_map(
        body, mesh=mesh, in_specs=placed, out_specs=P("shot", "tile", None), check_vma=False
    )
```

```python
import functools
import jax
import jax.numpy as jnp
import numpy as np
from jax import lax
from jax.experimental import pallas as pl
from jax.experimental.pallas import tpu as pltpu
from jax.sharding import PartitionSpec as P

MESH_ID = pl.DeviceIdType.MESH
SCALE = 5040.0
WEIGHTS = (-43050.0, 8064.0, -1008.0, 128.0, -9.0)
CENTRES = (-43008.0, -42.0)
NY, NX, NZ = 96, 32, 128
PY = 104
PX = 104
WIDE = 4
CHUNK = 128


def band_matrix(size, centre):
    band = centre * np.eye(size, dtype=np.float32)
    for offset in range(1, 5):
        band += WEIGHTS[offset] * (np.eye(size, k=offset) + np.eye(size, k=-offset))
    return band


def band_pair():
    deep, wide = band_matrix(NZ, CENTRES[0]), band_matrix(NY, CENTRES[1])
    deep = np.kron(np.eye(2, dtype=np.float32), deep)
    return (jnp.asarray(np.concatenate([deep, deep], axis=0), jnp.bfloat16),
            jnp.asarray(np.concatenate([wide, wide], axis=1), jnp.bfloat16))


def position():
    s = lax.axis_index("shot")
    t = lax.axis_index("tile")
    return s // 8, (s // 2) % 4, s % 2, t // 2, t % 2


def device(xh, y, core, z, xl):
    return (xh * 8 + y * 2 + core, z * 2 + xl)


def meet(xh, y, core, z, xl, more=None, wanted=None):
    barrier = pltpu.get_barrier_semaphore()
    peers = []
    for a in range(2):
        for b in range(2):
            for e in range(2):
                if a or b or e:
                    peers.append(device((xh + a) % 2, y, (core + b) % 2, z, (xl + e) % 2))
    for d in range(1, 4):
        peers.append(device(xh, (y + d) % 4, core, z, xl))
    for peer in peers:
        pl.semaphore_signal(barrier, inc=1, device_id=peer, device_id_type=MESH_ID)
    if more is None:
        pl.semaphore_wait(barrier, len(peers))
    else:
        @pl.when(wanted)
        def _():
            pl.semaphore_signal(barrier, inc=1, device_id=more, device_id_type=MESH_ID)
        pl.semaphore_wait(barrier, len(peers) + wanted.astype(jnp.int32))


def wave_kernel(blocks, model, fwd, adj, extra_in, band_z, band_y, out, *scratch):
    fields = (scratch[0:6], scratch[6:12])
    Z = scratch[12:14]
    (A, C, E, T, image, raw_f, raw_a, extra, line, packed, ring, ssem, rsem,
     xsend, xrecv, fsend, ysend, yrecv, msend, mrecv, local) = scratch[14:]
    xh, y, core, z, xl = position()
    place = 2 * z + core
    has_left = place > 0
    has_right = place < 7
    left = device(xh, y, 1 - core, z - 1 + core, xl)
    right = device(xh, y, 1 - core, z + core, xl)
    beyond = device(xh, y, 1 - core, z - 1 + 2 * core, xl)
    meet(xh, y, core, z, xl, beyond, (z - 1 + 2 * core >= 0) & (z - 1 + 2 * core < 4))
    away = core != xl
    home = core == xl

    def remote(source, target, send, recv, peer):
        return pltpu.make_async_remote_copy(src_ref=source, dst_ref=target, send_sem=send, recv_sem=recv,
                                            device_id=peer, device_id_type=MESH_ID)

    def own(k, peer):
        return remote(model, line.at[xh, core], xsend.at[k], xrecv.at[xh, core], peer)

    cross = own(0, device(1 - xh, y, xl, z, 1 - xl))
    pair = own(1, device(xh, y, xl, z, 1 - xl))
    inside = own(2, device(xh, y, 1 - core, z, xl))
    keep = pltpu.make_async_copy(model, line.at[xh, core], local.at[0])
    pair.start()
    cross.start()
    pl.when(away)(inside.start)
    pl.when(home)(keep.start)

    partner = device(xh, y, xl, z, core)
    moves = []
    for k, (source, target) in enumerate(((extra_in, extra), (fwd, raw_f), (adj, raw_a))):
        moves.append((remote(source, target, msend.at[k], mrecv.at[k], partner),
                      pltpu.make_async_copy(source, target, local.at[1 + k])))
    for far, near in moves:
        pl.when(away)(far.start)
        pl.when(home)(near.start)

    def arrived(a, b):
        remote(line.at[a, b], line.at[a, b], xsend.at[0], xrecv.at[a, b], partner).wait_recv()

    def forward(b):
        return remote(line.at[xh, b], line.at[xh, b], fsend.at[b], xrecv.at[xh, b],
                      device(1 - xh, y, core, z, 1 - xl))

    @pl.when(away)
    def _():
        for b in range(2):
            arrived(xh, b)
            forward(b).start()

    @pl.when(home)
    def _():
        keep.wait()
        arrived(xh, 1 - core)

    for b in range(2):
        arrived(1 - xh, b)

    def pick(target, d):
        first = blocks[xh * 8 + ((y + d) % 4) * 2 + xl]
        for b in range(2):
            half = (2 * y + b < first).astype(jnp.int32)

            def rows(i, carry):
                part = pl.ds(pl.multiple_of(64 * i, 64), 64)
                target[b, :, part, :] = line[half, b, :, part, :]
                return carry
            lax.fori_loop(0, 8, rows, 0)

    def round_trip(d):
        return remote(packed.at[d - 1], ring.at[d], ysend.at[d - 1], yrecv.at[d - 1],
                      device(xh, (y + d) % 4, core, z, xl))

    for d in (2, 1, 3):
        pick(packed.at[d - 1], d)
        round_trip(d).start()
    def landed(i):
        far, near = moves[i]
        pl.when(away)(far.wait_recv)
        pl.when(home)(near.wait)

    def halo(f, slot, par, side):
        if side == 0:
            return pltpu.make_async_remote_copy(
                src_ref=fields[f][slot].at[pl.ds(4, 4), pl.ds(0, NY), :],
                dst_ref=fields[f][slot].at[pl.ds(36, 4), pl.ds(0, NY), :],
                send_sem=ssem.at[f, 0, par], recv_sem=rsem.at[f, 0, par],
                device_id=left, device_id_type=MESH_ID)
        return pltpu.make_async_remote_copy(
            src_ref=fields[f][slot].at[pl.ds(32, 4), pl.ds(0, NY), :],
            dst_ref=fields[f][slot].at[pl.ds(0, 4), pl.ds(0, NY), :],
            send_sem=ssem.at[f, 1, par], recv_sem=rsem.at[f, 1, par],
            device_id=right, device_id_type=MESH_ID)

    def send(f, slot, par, side):
        @pl.when(has_left if side == 0 else has_right)
        def _():
            halo(f, slot, par, side).start()

    def wait(f, slot, par):
        @pl.when(has_left)
        def _():
            halo(f, slot, par, 0).wait_send()
            halo(f, slot, par, 1).wait_recv()

        @pl.when(has_right)
        def _():
            halo(f, slot, par, 1).wait_send()
            halo(f, slot, par, 0).wait_recv()

    zero_side = jnp.zeros((4, NY, NZ), jnp.float32)

    @pl.when(place == 0)
    def _():
        for f in range(2):
            for slot in range(6):
                fields[f][slot][pl.ds(0, 4), pl.ds(0, NY), :] = zero_side

    @pl.when(place == 7)
    def _():
        for f in range(2):
            for slot in range(6):
                fields[f][slot][pl.ds(36, 4), pl.ds(0, NY), :] = zero_side

    landed(0)
    lane = lax.broadcasted_iota(jnp.int32, (8, NZ), 1)
    row = lax.broadcasted_iota(jnp.int32, (8, NZ), 0)
    depth = jnp.broadcast_to(extra[pl.ds(192, 8), pl.ds(9, 1)], (8, NZ))
    plane = jnp.where(lane.astype(jnp.float32) == depth, 0.5, 0.0)
    cell = jnp.broadcast_to(extra[pl.ds(192, 8), pl.ds(8, 1)], (8, NZ))
    turns = [(depth + m) - jnp.where(depth + m >= NZ, float(NZ), 0.0) for m in range(8)]

    def load_extra(j, carry):
        rows = pl.ds(pl.multiple_of(8 * j, 8), 8)
        records = [extra[pl.ds(pl.multiple_of(NY * h + 8 * j, 8), 8), :] for h in range(2)]
        for x in range(NX):
            placed = jnp.zeros((8, NZ), jnp.float32)
            for m in range(8):
                at = (m % 4) * NX + x
                value = jnp.broadcast_to(records[m // 4][:, at:at + 1], (8, NZ))
                placed = jnp.where(lane.astype(jnp.float32) == turns[m], value, placed)
            T[x, rows, :] = placed
            index = (place * NX + x) * (NY * NZ) + (row + 8 * j) * NZ + lane
            E[x, rows, :] = jnp.where(index.astype(jnp.float32) == cell, 0.5, 0.0)
            image[x, rows, :] = jnp.zeros((8, NZ), jnp.float32)
        return carry

    lax.fori_loop(0, NY // 8, load_extra, 0)

    def load_states(f, source):
        def tiles(j, carry):
            rows = pl.ds(pl.multiple_of(8 * j, 8), 8)
            for x in range(NX):
                picked = pl.ds(8 * NX * j + x, 8, stride=NX)
                fields[f][1][4 + x, rows, :] = source[0, picked, :]
                fields[f][0][4 + x, rows, :] = source[1, picked, :]
            return carry
        lax.fori_loop(0, NY // 8, tiles, 0)
        send(f, 1, 0, 0)
        send(f, 1, 0, 1)

    def across(f, slot, x):
        for h in range(0, WIDE, 2):
            u = fields[f][slot][pl.ds(4 + x + h, 2), pl.ds(0, NY), :]
            high = u.astype(jnp.bfloat16)
            low = (u - high.astype(jnp.float32)).astype(jnp.bfloat16)
            high = jnp.concatenate([high[0], high[1]], axis=1)
            low = jnp.concatenate([low[0], low[1]], axis=1)
            rows = jnp.concatenate([high, low, band_y[...]], axis=1)
            columns = jnp.concatenate([band_z[...], high, low], axis=0)
            both = jnp.dot(rows, columns, preferred_element_type=jnp.float32)
            Z[f][x + h, pl.ds(0, NY), :] = both[:, :NZ]
            Z[f][x + h + 1, pl.ds(0, NY), :] = both[:, NZ:]

    def slot_of(n):
        return n + 1 if n < 5 else (n + 1) % 2

    def advance(f, n):
        cur, prev, new = fields[f][slot_of(n - 1)], fields[f][slot_of(n - 2)], fields[f][slot_of(n)]
        other = fields[1 - f][slot_of(9 - n)] if n > 4 else None
        wait(f, slot_of(n - 1), (n - 1) % 2)
        amp = jnp.broadcast_to(extra[pl.ds(192, 8), pl.ds(n - 1, 1)], (8, NZ))

        def planes(i, carry):
            x = WIDE * i
            if f == 0 and n > 1:
                across(1, slot_of(n - 1), x)
            if f == 1 and n < 8:
                across(0, slot_of(n), x)
            for j in range(NY // 8):
                rows = pl.ds(8 * j, 8)
                wide = cur[pl.ds(x, WIDE + 8), rows, :]
                u = wide[4:4 + WIDE]
                acc = Z[f][pl.ds(x, WIDE), rows, :]
                for k in range(1, 5):
                    acc = acc + WEIGHTS[k] * (wide[4 + k:4 + k + WIDE] + wide[4 - k:4 - k + WIDE])
                v = prev[pl.ds(4 + x, WIDE), rows, :]
                if f == 0:
                    force = E[pl.ds(x, WIDE), rows, :] * amp[None]
                else:
                    force = jnp.stack([pltpu.roll(T[x + h, rows, :], NZ - (8 - n), 1) * plane for h in range(WIDE)])
                w = v + A[pl.ds(x, WIDE), rows, :] * ((u - v) + (C[pl.ds(x, WIDE), rows, :] * acc + force))
                new[pl.ds(4 + x, WIDE), rows, :] = w
                if other is not None:
                    image[pl.ds(x, WIDE), rows, :] += w * other[pl.ds(4 + x, WIDE), rows, :]
            return carry

        for first, last, side in ((0, 4 // WIDE, 0), (28 // WIDE, 32 // WIDE, 1), (4 // WIDE, 28 // WIDE, None)):
            lax.fori_loop(first, last, planes, 0)
            if side is not None and n < 8:
                send(f, slot_of(n), n % 2, side)

    def first_across(f):
        def planes(i, carry):
            across(f, 1, WIDE * i)
            return carry
        lax.fori_loop(0, NX // WIDE, planes, 0)

    landed(1)
    load_states(0, raw_f)
    first_across(0)
    pick(ring.at[0], 0)
    for d in (1, 3, 2):
        round_trip(d).wait()


    first = blocks[xh * 8 + y * 2 + xl]

    def load_model(k, carry):
        j = first + k
        turn = (y - (j // 2) % 4 + 4) % 4
        parity = j % 2
        for h in range(2):
            rows = pl.ds(pl.multiple_of(16 * k + 8 * h, 8), 8)
            for x in range(NX):
                picked = pl.ds(8 * NX * h + x, 8, stride=NX)
                A[x, rows, :] = 2.0 / (1.0 + ring[turn, parity, 1, picked, :])
                C[x, rows, :] = ring[turn, parity, 0, picked, :] * (0.5 / SCALE)
        return carry

    lax.fori_loop(0, 6, load_model, 0)
    advance(0, 1)
    landed(2)
    load_states(1, raw_a)
    first_across(1)
    for n in range(1, 9):
        advance(1, n)
        if n < 8:
            advance(0, n + 1)

    def store(j, carry):
        rows = pl.ds(pl.multiple_of(8 * j, 8), 8)
        for x in range(NX):
            out[pl.ds(8 * NX * j + x, 8, stride=NX), :] = image[x, rows, :] * 0.125
        return carry

    lax.fori_loop(0, NY // 8, store, 0)

    pair.wait_send()
    cross.wait_send()

    @pl.when(away)
    def _():
        inside.wait_send()
        for b in range(2):
            forward(b).wait_send()
        for far, near in moves:
            far.wait_send()


def run_wave(blocks, model, fwd, adj, extra):
    vm = pl.BlockSpec(memory_space=pltpu.VMEM)
    anywhere = pl.BlockSpec(memory_space=pl.ANY)
    dma = pltpu.SemaphoreType.DMA
    full = lambda: pltpu.VMEM((NX, PX, NZ), jnp.float32)
    return pl.pallas_call(
        wave_kernel,
        out_shape=jax.ShapeDtypeStruct((NY * NX, NZ), jnp.float32),
        in_specs=[pl.BlockSpec(memory_space=pltpu.SMEM)] + [anywhere] * 4 + [vm] * 2,
        out_specs=vm,
        scratch_shapes=[
            *[pltpu.VMEM((NX + 8, PY, NZ), jnp.float32) for _ in range(12)],
            *[full() for _ in range(7)],
            pltpu.VMEM((2, NY * NX, NZ), jnp.float32),
            pltpu.VMEM((2, NY * NX, NZ), jnp.float32),
            pltpu.VMEM((2 * NY + 8, NZ), jnp.float32),
            pltpu.VMEM((2, 2, 2, 512, NZ), jnp.float32),
            pltpu.VMEM((3, 2, 2, 512, NZ), jnp.float32),
            pltpu.VMEM((4, 2, 2, 512, NZ), jnp.float32),
            dma((2, 2, 2)), dma((2, 2, 2)),
            dma((3,)), dma((2, 2)), dma((2,)), dma((3,)), dma((3,)), dma((3,)), dma((3,)), dma((4,)),
        ],
        compiler_params=pltpu.CompilerParams(collective_id=1, has_side_effects=True, vmem_limit_bytes=61 << 20),
        name="wave_steps",
    )(blocks, model, fwd, adj, extra, *band_pair())


def sum_kernel(blocks, partial, out, packed, ring, totals, line, ysend, yrecv, xsend, xrecv):
    xh, y, core, z, xl = position()
    meet(xh, y, core, z, xl)

    def choose(first, row, b):
        half = (2 * row + b < first).astype(jnp.int32)
        step = 8 * half + 2 * row + b - first
        inside = (step >= 0).astype(jnp.int32) * (step < 6).astype(jnp.int32)
        return half + 2 * (1 - inside), step

    def turn(d, q):
        return pltpu.make_async_remote_copy(
            src_ref=packed.at[q, d - 1], dst_ref=ring.at[q, d], send_sem=ysend.at[q, d - 1], recv_sem=yrecv.at[q, d - 1],
            device_id=device(xh, (y + d) % 4, core, z, xl), device_id_type=MESH_ID)

    def pick(target, d, q):
        first = blocks[xh * 8 + y * 2 + xl]
        for b in range(2):
            half, step = choose(first, (y + d) % 4, b)
            target[b] = partial[jnp.clip(step, 0, 5), pl.ds(CHUNK * q, CHUNK), :]

    for q in range(512 // CHUNK):
        for d in (2, 1, 3):
            pick(packed.at[q, d - 1], d, q)
            turn(d, q).start()
        pick(ring.at[q, 0], 0, q)

    def spread(k, q):
        a, b = k // 2, k % 2
        return pltpu.make_async_remote_copy(
            src_ref=totals.at[q, k], dst_ref=line.at[q, xh * 2 + xl], send_sem=xsend.at[q, k],
            recv_sem=xrecv.at[q, xh * 2 + xl], device_id=device(a, y, b, z, core), device_id_type=MESH_ID)

    def mine(k):
        return (xh == k // 2) & (core == k % 2) & (xl == core)

    for q in range(512 // CHUNK):
        for d in (1, 3, 2):
            turn(d, q).wait_recv()
        for k in range(4):
            a, b = k // 2, k % 2
            total = jnp.zeros((CHUNK, NZ), jnp.float32)
            for d in range(4):
                first = blocks[xh * 8 + ((y - d + 4) % 4) * 2 + xl]
                half, step = choose(first, y, b)
                total = total + jnp.where(jnp.full((CHUNK, NZ), half, jnp.int32) == a, ring[q, d, b], 0.0)
            totals[q, k] = total

            @pl.when(jnp.logical_not(mine(k)))
            def _():
                spread(k, q).start()

            @pl.when(mine(k))
            def _():
                line[q, xh * 2 + xl] = totals[q, k]

    for q in range(512 // CHUNK):
        for k in range(4):
            source = device(k // 2, y, xl, z, k % 2)

            @pl.when(jnp.logical_not((xh * 2 + xl == k) & (xl == core)))
            def _():
                pltpu.make_async_remote_copy(
                    src_ref=line.at[q, k], dst_ref=line.at[q, k], send_sem=xsend.at[q, k], recv_sem=xrecv.at[q, k],
                    device_id=source, device_id_type=MESH_ID).wait_recv()
        out[pl.ds(CHUNK * q, CHUNK), :] = (line[q, 0] + line[q, 1]) + (line[q, 2] + line[q, 3])

    for q in range(512 // CHUNK):
        for d in (1, 3, 2):
            turn(d, q).wait_send()
        for k in range(4):
            @pl.when(jnp.logical_not(mine(k)))
            def _():
                spread(k, q).wait_send()


def run_sum(blocks, partial):
    vm = pl.BlockSpec(memory_space=pltpu.VMEM)
    dma = pltpu.SemaphoreType.DMA
    count = 512 // CHUNK
    return pl.pallas_call(
        sum_kernel,
        out_shape=jax.ShapeDtypeStruct((512, NZ), jnp.float32),
        in_specs=[pl.BlockSpec(memory_space=pltpu.SMEM), vm],
        out_specs=vm,
        scratch_shapes=[
            pltpu.VMEM((count, 3, 2, CHUNK, NZ), jnp.float32),
            pltpu.VMEM((count, 4, 2, CHUNK, NZ), jnp.float32),
            pltpu.VMEM((count, 4, CHUNK, NZ), jnp.float32),
            pltpu.VMEM((count, 4, CHUNK, NZ), jnp.float32),
            dma((count, 3)), dma((count, 3)), dma((count, 4)), dma((count, 4)),
        ],
        compiler_params=pltpu.CompilerParams(collective_id=3, has_side_effects=True, vmem_limit_bytes=24 << 20),
        name="image_sum",
    )(blocks, partial)


def body(courant, damping, aperture_block, source_cell, receiver_depth, wavelet, receiver_data,
         forward_state, adjoint_state):
    records = receiver_data[0].reshape(2, 4, NY, NX).transpose(0, 2, 1, 3).reshape(2 * NY, NZ)
    misc = jnp.concatenate([wavelet[0], source_cell.astype(jnp.float32), receiver_depth.astype(jnp.float32),
                            jnp.zeros((NZ - 10,), jnp.float32)])
    extra = jnp.concatenate([records, jnp.broadcast_to(misc[None], (8, NZ))], axis=0)
    model = jnp.stack([courant.reshape(512, NZ), damping.reshape(512, NZ)])
    partial = run_wave(aperture_block, model, forward_state[0].reshape(2, NY * NX, NZ),
                       adjoint_state[0].reshape(2, NY * NX, NZ), extra).reshape(6, 512, NZ)
    return run_sum(aperture_block, partial).reshape(16, NX, NZ)


def solution(mesh):
    placed = (
        P("shot", "tile", None),
        P("shot", "tile", None),
        P(),
        P("shot"),
        P("shot"),
        P("shot", None),
        P("shot", None, None, "tile"),
        P("shot", None, None, "tile", None),
        P("shot", None, None, "tile", None),
    )
    return jax.shard_map(
        body, mesh=mesh, in_specs=placed, out_specs=P("shot", "tile", None), check_vma=False
    )
```

```python
import functools
import jax
import jax.numpy as jnp
import numpy as np
from jax import lax
from jax.experimental import pallas as pl
from jax.experimental.pallas import tpu as pltpu
from jax.sharding import PartitionSpec as P

MESH_ID = pl.DeviceIdType.MESH
SCALE = 5040.0
WEIGHTS = (-43050.0, 8064.0, -1008.0, 128.0, -9.0)
CENTRES = (-43008.0, -42.0)
NY, NX, NZ = 96, 32, 128
PY = 104
PX = 104
WIDE = 4
CHUNK = 128


def band_matrix(size, centre):
    band = centre * np.eye(size, dtype=np.float32)
    for offset in range(1, 5):
        band += WEIGHTS[offset] * (np.eye(size, k=offset) + np.eye(size, k=-offset))
    return band


def band_pair():
    deep, wide = band_matrix(NZ, CENTRES[0]), band_matrix(NY, CENTRES[1])
    deep = np.kron(np.eye(2, dtype=np.float32), deep)
    return (jnp.asarray(np.concatenate([deep, deep], axis=0), jnp.bfloat16),
            jnp.asarray(np.concatenate([wide, wide], axis=1), jnp.bfloat16))


def position():
    s = lax.axis_index("shot")
    t = lax.axis_index("tile")
    return s // 8, (s // 2) % 4, s % 2, t // 2, t % 2


def device(xh, y, core, z, xl):
    return (xh * 8 + y * 2 + core, z * 2 + xl)


def meet(xh, y, core, z, xl, more, wanted, between):
    barrier = pltpu.get_barrier_semaphore()
    peers = []
    for a in range(2):
        for b in range(2):
            for e in range(2):
                if a or b or e:
                    peers.append(device((xh + a) % 2, y, (core + b) % 2, z, (xl + e) % 2))
    for d in range(1, 4):
        peers.append(device(xh, (y + d) % 4, core, z, xl))
    for peer in peers:
        pl.semaphore_signal(barrier, inc=1, device_id=peer, device_id_type=MESH_ID)
    @pl.when(wanted)
    def _():
        pl.semaphore_signal(barrier, inc=1, device_id=more, device_id_type=MESH_ID)
    between()
    pl.semaphore_wait(barrier, len(peers) + wanted.astype(jnp.int32))


def wave_kernel(blocks, wavelet, cell_in, depth_in, courant, damping, fwd, adj, records_in, band_z, band_y, out, *scratch):
    fields = (scratch[0:6], scratch[6:12])
    Z = scratch[12:14]
    (A, C, E, T, image, raw_f, raw_a, extra_in, extra, line, packed, ring, turned, lined, ssem, rsem,
     xsend, xrecv, fsend, ysend, yrecv, msend, mrecv, local, isend, irecv, osend, orecv) = scratch[14:]
    xh, y, core, z, xl = position()
    place = 2 * z + core
    has_left = place > 0
    has_right = place < 7
    left = device(xh, y, 1 - core, z - 1 + core, xl)
    right = device(xh, y, 1 - core, z + core, xl)
    beyond = device(xh, y, 1 - core, z - 1 + 2 * core, xl)
    lane = lax.broadcasted_iota(jnp.int32, (8, NZ), 1)
    row = lax.broadcasted_iota(jnp.int32, (8, NZ), 0)

    def pack():
        for h in range(2):
            extra_in[pl.ds(NY * h, NY), :] = jnp.concatenate([records_in[4 * h + m] for m in range(4)], axis=1)
        misc = jnp.zeros((8, NZ), jnp.float32)
        for m in range(8):
            misc = jnp.where(lane == m, wavelet[0, m], misc)
        misc = jnp.where(lane == 8, cell_in[0].astype(jnp.float32), misc)
        extra_in[pl.ds(2 * NY, 8), :] = jnp.where(lane == 9, depth_in[0].astype(jnp.float32), misc)

    meet(xh, y, core, z, xl, beyond, (z - 1 + 2 * core >= 0) & (z - 1 + 2 * core < 4), pack)
    away = core != xl
    home = core == xl

    def remote(source, target, send, recv, peer):
        return pltpu.make_async_remote_copy(src_ref=source, dst_ref=target, send_sem=send, recv_sem=recv,
                                            device_id=peer, device_id_type=MESH_ID)

    model = (courant, damping)

    def own(k, peer):
        return [remote(model[a], line.at[xh, core, a], xsend.at[k, a], xrecv.at[xh, core, a], peer) for a in range(2)]

    cross = own(0, device(1 - xh, y, xl, z, 1 - xl))
    pair = own(1, device(xh, y, xl, z, 1 - xl))
    inside = own(2, device(xh, y, 1 - core, z, xl))
    keep = [pltpu.make_async_copy(model[a], line.at[xh, core, a], local.at[a]) for a in range(2)]
    for a in range(2):
        pair[a].start()
        cross[a].start()
        pl.when(away)(inside[a].start)
        pl.when(home)(keep[a].start)

    partner = device(xh, y, xl, z, core)
    moves = []
    for k, (source, target) in enumerate(((extra_in, extra), (fwd, raw_f), (adj.at[1], raw_a.at[1]), (adj.at[0], raw_a.at[0]))):
        moves.append((remote(source, target, msend.at[k], mrecv.at[k], partner),
                      pltpu.make_async_copy(source, target, local.at[2 + k])))
    for far, near in moves:
        pl.when(away)(far.start)
        pl.when(home)(near.start)

    def arrived(a, b):
        for e in range(2):
            remote(line.at[a, b, e], line.at[a, b, e], xsend.at[0, e], xrecv.at[a, b, e], partner).wait_recv()

    def forward(b):
        return [remote(line.at[xh, b, a], line.at[xh, b, a], fsend.at[b, a], xrecv.at[xh, b, a],
                       device(1 - xh, y, core, z, 1 - xl)) for a in range(2)]

    @pl.when(away)
    def _():
        for b in range(2):
            arrived(xh, b)
            for copy in forward(b):
                copy.start()

    @pl.when(home)
    def _():
        for copy in keep:
            copy.wait()
        arrived(xh, 1 - core)

    for b in range(2):
        arrived(1 - xh, b)

    def pick(target, d):
        first = blocks[xh * 8 + ((y + d) % 4) * 2 + xl]
        for b in range(2):
            half = (2 * y + b < first).astype(jnp.int32)

            def rows(i, carry):
                part = pl.ds(pl.multiple_of(64 * i, 64), 64)
                target[b, :, part, :] = line[half, b, :, part, :]
                return carry
            lax.fori_loop(0, 8, rows, 0)

    def round_trip(d):
        return remote(packed.at[d - 1], ring.at[d], ysend.at[d - 1], yrecv.at[d - 1],
                      device(xh, (y + d) % 4, core, z, xl))

    for d in (2, 1, 3):
        pick(packed.at[d - 1], d)
        round_trip(d).start()
    def landed(i):
        far, near = moves[i]
        pl.when(away)(far.wait_recv)
        pl.when(home)(near.wait)

    def halo(f, slot, par, side):
        if side == 0:
            return pltpu.make_async_remote_copy(
                src_ref=fields[f][slot].at[pl.ds(4, 4), pl.ds(0, NY), :],
                dst_ref=fields[f][slot].at[pl.ds(36, 4), pl.ds(0, NY), :],
                send_sem=ssem.at[f, 0, par], recv_sem=rsem.at[f, 0, par],
                device_id=left, device_id_type=MESH_ID)
        return pltpu.make_async_remote_copy(
            src_ref=fields[f][slot].at[pl.ds(32, 4), pl.ds(0, NY), :],
            dst_ref=fields[f][slot].at[pl.ds(0, 4), pl.ds(0, NY), :],
            send_sem=ssem.at[f, 1, par], recv_sem=rsem.at[f, 1, par],
            device_id=right, device_id_type=MESH_ID)

    def send(f, slot, par, side):
        @pl.when(has_left if side == 0 else has_right)
        def _():
            halo(f, slot, par, side).start()

    def wait(f, slot, par):
        @pl.when(has_left)
        def _():
            halo(f, slot, par, 0).wait_send()
            halo(f, slot, par, 1).wait_recv()

        @pl.when(has_right)
        def _():
            halo(f, slot, par, 1).wait_send()
            halo(f, slot, par, 0).wait_recv()

    zero_side = jnp.zeros((4, NY, NZ), jnp.float32)

    @pl.when(place == 0)
    def _():
        for f in range(2):
            for slot in range(6):
                fields[f][slot][pl.ds(0, 4), pl.ds(0, NY), :] = zero_side

    @pl.when(place == 7)
    def _():
        for f in range(2):
            for slot in range(6):
                fields[f][slot][pl.ds(36, 4), pl.ds(0, NY), :] = zero_side

    landed(0)
    depth = jnp.broadcast_to(extra[pl.ds(192, 8), pl.ds(9, 1)], (8, NZ))
    plane = jnp.where(lane.astype(jnp.float32) == depth, 0.5, 0.0)
    cell = jnp.broadcast_to(extra[pl.ds(192, 8), pl.ds(8, 1)], (8, NZ))
    turns = [(depth + m) - jnp.where(depth + m >= NZ, float(NZ), 0.0) for m in range(8)]

    def load_extra(j, carry):
        rows = pl.ds(pl.multiple_of(8 * j, 8), 8)
        records = [extra[pl.ds(pl.multiple_of(NY * h + 8 * j, 8), 8), :] for h in range(2)]
        for x in range(NX):
            placed = jnp.zeros((8, NZ), jnp.float32)
            for m in range(8):
                at = (m % 4) * NX + x
                value = jnp.broadcast_to(records[m // 4][:, at:at + 1], (8, NZ))
                placed = jnp.where(lane.astype(jnp.float32) == turns[m], value, placed)
            T[x, rows, :] = placed
            index = (place * NX + x) * (NY * NZ) + (row + 8 * j) * NZ + lane
            E[x, rows, :] = jnp.where(index.astype(jnp.float32) == cell, 0.5, 0.0)
        return carry

    lax.fori_loop(0, NY // 8, load_extra, 0)

    def clear(x, carry):
        image[x] = jnp.zeros((6, 16, NZ), jnp.float32)
        return carry

    lax.fori_loop(0, NX, clear, 0)

    def load_state(f, slot, source):
        def planes(picks):
            def tiles(j, carry):
                rows = pl.ds(pl.multiple_of(8 * j, 8), 8)
                for x in picks:
                    fields[f][slot][4 + x, rows, :] = source[pl.ds(8 * NX * j + x, 8, stride=NX), :]
                return carry
            lax.fori_loop(0, NY // 8, tiles, 0)

        planes([*range(4), *range(28, 32)])
        if slot == 1:
            send(f, 1, 0, 0)
            send(f, 1, 0, 1)
        planes(range(4, 28))

    def across(f, slot, x):
        for h in range(0, WIDE, 2):
            u = fields[f][slot][pl.ds(4 + x + h, 2), pl.ds(0, NY), :]
            high = u.astype(jnp.bfloat16)
            low = (u - high.astype(jnp.float32)).astype(jnp.bfloat16)
            high = jnp.concatenate([high[0], high[1]], axis=1)
            low = jnp.concatenate([low[0], low[1]], axis=1)
            rows = jnp.concatenate([high, low, band_y[...]], axis=1)
            columns = jnp.concatenate([band_z[...], high, low], axis=0)
            both = jnp.dot(rows, columns, preferred_element_type=jnp.float32)
            Z[f][x + h, pl.ds(0, NY), :] = both[:, :NZ]
            Z[f][x + h + 1, pl.ds(0, NY), :] = both[:, NZ:]

    def slot_of(n):
        return n + 1 if n < 5 else (n + 1) % 2

    def advance(f, n):
        cur, prev, new = fields[f][slot_of(n - 1)], fields[f][slot_of(n - 2)], fields[f][slot_of(n)]
        other = fields[1 - f][slot_of(9 - n)] if n > 4 else None
        late = f == 1 and n == 1
        if not late:
            wait(f, slot_of(n - 1), (n - 1) % 2)
        amp = jnp.broadcast_to(extra[pl.ds(192, 8), pl.ds(n - 1, 1)], (8, NZ))

        def planes(i, carry):
            x = WIDE * i
            if f == 0 and n > 1:
                across(1, slot_of(n - 1), x)
            if f == 1 and n < 8:
                across(0, slot_of(n), x)
            for j in range(NY // 8):
                rows = pl.ds(8 * j, 8)
                wide = cur[pl.ds(x, WIDE + 8), rows, :]
                u = wide[4:4 + WIDE]
                acc = Z[f][pl.ds(x, WIDE), rows, :]
                for k in range(1, 5):
                    acc = acc + WEIGHTS[k] * (wide[4 + k:4 + k + WIDE] + wide[4 - k:4 - k + WIDE])
                v = prev[pl.ds(4 + x, WIDE), rows, :]
                if f == 0:
                    force = E[pl.ds(x, WIDE), rows, :] * amp[None]
                else:
                    force = jnp.stack([pltpu.roll(T[x + h, rows, :], NZ - (8 - n), 1) * plane for h in range(WIDE)])
                w = v + A[pl.ds(x, WIDE), rows, :] * ((u - v) + (C[pl.ds(x, WIDE), rows, :] * acc + force))
                new[pl.ds(4 + x, WIDE), rows, :] = w
                if other is not None:
                    image[pl.ds(x, WIDE), j // 2, pl.ds(8 * (j % 2), 8), :] += w * other[pl.ds(4 + x, WIDE), rows, :]
            return carry

        parts = [(0, 4 // WIDE, 0), (28 // WIDE, 32 // WIDE, 1), (4 // WIDE, 28 // WIDE, None)]
        for first, last, side in (parts[2:] + parts[:2] if late else parts):
            if late and side == 0:
                wait(f, slot_of(n - 1), (n - 1) % 2)
            lax.fori_loop(first, last, planes, 0)
            if side is not None and n < 8:
                send(f, slot_of(n), n % 2, side)

    def first_across(f):
        def planes(i, carry):
            across(f, 1, WIDE * i)
            return carry
        lax.fori_loop(0, NX // WIDE, planes, 0)

    landed(1)
    load_state(0, 1, raw_f.at[0])
    load_state(0, 0, raw_f.at[1])
    first_across(0)
    pick(ring.at[0], 0)
    for d in (1, 3, 2):
        round_trip(d).wait()


    first = blocks[xh * 8 + y * 2 + xl]

    def load_model(k, carry):
        j = first + k
        turn = (y - (j // 2) % 4 + 4) % 4
        parity = j % 2
        for h in range(2):
            rows = pl.ds(pl.multiple_of(16 * k + 8 * h, 8), 8)
            for x in range(NX):
                picked = pl.ds(8 * NX * h + x, 8, stride=NX)
                A[x, rows, :] = 2.0 / (1.0 + ring[turn, parity, 1, picked, :])
                C[x, rows, :] = ring[turn, parity, 0, picked, :] * (0.5 / SCALE)
        return carry

    lax.fori_loop(0, 6, load_model, 0)
    advance(0, 1)
    landed(2)
    load_state(1, 0, raw_a.at[1])
    landed(3)
    load_state(1, 1, raw_a.at[0])
    first_across(1)
    for n in range(1, 9):
        advance(1, n)
        if n < 8:
            advance(0, n + 1)

    def choose(first, row, b):
        half = (2 * row + b < first).astype(jnp.int32)
        step = 8 * half + 2 * row + b - first
        inside = (step >= 0).astype(jnp.int32) * (step < 6).astype(jnp.int32)
        return half + 2 * (1 - inside), step

    def packet(d, q):
        return raw_f.at[0, pl.ds(256 * (3 * q + d - 1), 256), :]

    def total_of(k, q):
        return raw_f.at[1, pl.ds(CHUNK * (4 * q + k), CHUNK), :]

    def turn(d, q):
        return remote(packet(d, q), turned.at[q, d], isend.at[q, d - 1], irecv.at[q, d - 1],
                      device(xh, (y + d) % 4, core, z, xl))

    def pick_image(target, d, q):
        for b in range(2):
            half, step = choose(first, (y + d) % 4, b)
            value = image[pl.ds(8 * q, 8), jnp.clip(step, 0, 5), :, :] * 0.125
            target[pl.ds(CHUNK * b, CHUNK), :] = value.reshape(CHUNK, NZ)

    for q in range(4):
        for d in (2, 1, 3):
            pick_image(packet(d, q), d, q)
            turn(d, q).start()
        pick_image(turned.at[q, 0], 0, q)

    def spread(k, q):
        return remote(total_of(k, q), lined.at[q, xh * 2 + xl], osend.at[q, k], orecv.at[q, xh * 2 + xl],
                      device(k // 2, y, k % 2, z, core))

    def mine(k):
        return (xh == k // 2) & (core == k % 2) & (xl == core)

    for q in range(4):
        for d in (1, 3, 2):
            turn(d, q).wait_recv()
        for k in range(4):
            a, b = k // 2, k % 2
            total = jnp.zeros((CHUNK, NZ), jnp.float32)
            for d in range(4):
                half, step = choose(blocks[xh * 8 + ((y - d + 4) % 4) * 2 + xl], y, b)
                part = turned[q, d, pl.ds(CHUNK * b, CHUNK), :]
                total = total + jnp.where(jnp.full((CHUNK, NZ), half, jnp.int32) == a, part, 0.0)
            total_of(k, q)[...] = total

            @pl.when(jnp.logical_not(mine(k)))
            def _():
                spread(k, q).start()

            @pl.when(mine(k))
            def _():
                lined[q, xh * 2 + xl] = total_of(k, q)[...]

    for q in range(4):
        for k in range(4):
            @pl.when(jnp.logical_not((xh * 2 + xl == k) & (xl == core)))
            def _():
                remote(lined.at[q, k], lined.at[q, k], osend.at[q, k], orecv.at[q, k],
                       device(k // 2, y, xl, z, k % 2)).wait_recv()
        total = (lined[q, 0] + lined[q, 1]) + (lined[q, 2] + lined[q, 3])
        for i in range(8):
            for h in range(2):
                out[pl.ds(8 * NX * h + 8 * q + i, 8, stride=NX), :] = total[16 * i + 8 * h:16 * i + 8 * h + 8]

    for q in range(4):
        for d in (1, 3, 2):
            turn(d, q).wait_send()
        for k in range(4):
            @pl.when(jnp.logical_not(mine(k)))
            def _():
                spread(k, q).wait_send()

    for copy in pair + cross:
        copy.wait_send()

    @pl.when(away)
    def _():
        for copy in inside + forward(0) + forward(1):
            copy.wait_send()
        for far, near in moves:
            far.wait_send()


def run_wave(blocks, wavelet, cell, depth, courant, damping, fwd, adj, records):
    vm = pl.BlockSpec(memory_space=pltpu.VMEM)
    scalars = pl.BlockSpec(memory_space=pltpu.SMEM)
    anywhere = pl.BlockSpec(memory_space=pl.ANY)
    dma = pltpu.SemaphoreType.DMA
    full = lambda: pltpu.VMEM((NX, PX, NZ), jnp.float32)
    flat = lambda *shape: pltpu.VMEM((*shape, NZ), jnp.float32)
    return pl.pallas_call(
        wave_kernel,
        out_shape=jax.ShapeDtypeStruct((512, NZ), jnp.float32),
        in_specs=[scalars] * 4 + [anywhere] * 4 + [vm] * 3,
        out_specs=vm,
        scratch_shapes=[
            *[flat(NX + 8, PY) for _ in range(12)],
            *[full() for _ in range(6)],
            flat(NX, 6, 16),
            flat(2, NY * NX),
            flat(2, NY * NX),
            flat(2 * NY + 8),
            flat(2 * NY + 8),
            flat(2, 2, 2, 512),
            flat(3, 2, 2, 512),
            flat(4, 2, 2, 512),
            flat(4, 4, 256),
            flat(4, 4, CHUNK),
            dma((2, 2, 2)), dma((2, 2, 2)),
            dma((3, 2)), dma((2, 2, 2)), dma((2, 2)), dma((3,)), dma((3,)), dma((4,)), dma((4,)), dma((6,)),
            dma((4, 3)), dma((4, 3)), dma((4, 4)), dma((4, 4)),
        ],
        compiler_params=pltpu.CompilerParams(collective_id=1, has_side_effects=True, vmem_limit_bytes=61 << 20),
        name="wave_steps",
    )(blocks, wavelet, cell, depth, courant, damping, fwd, adj, records, *band_pair())


def body(courant, damping, aperture_block, source_cell, receiver_depth, wavelet, receiver_data,
         forward_state, adjoint_state):
    image = run_wave(aperture_block, wavelet, source_cell, receiver_depth, courant.reshape(512, NZ),
                     damping.reshape(512, NZ), forward_state[0].reshape(2, NY * NX, NZ),
                     adjoint_state[0].reshape(2, NY * NX, NZ), receiver_data[0])
    return image.reshape(16, NX, NZ)


def solution(mesh):
    placed = (
        P("shot", "tile", None),
        P("shot", "tile", None),
        P(),
        P("shot"),
        P("shot"),
        P("shot", None),
        P("shot", None, None, "tile"),
        P("shot", None, None, "tile", None),
        P("shot", None, None, "tile", None),
    )
    return jax.shard_map(
        body, mesh=mesh, in_specs=placed, out_specs=P("shot", "tile", None), check_vma=False
    )
```

```python
import functools
import jax
import jax.numpy as jnp
import numpy as np
from jax import lax
from jax.experimental import pallas as pl
from jax.experimental.pallas import tpu as pltpu
from jax.sharding import PartitionSpec as P

MESH_ID = pl.DeviceIdType.MESH
SCALE = 5040.0
WEIGHTS = (-43050.0, 8064.0, -1008.0, 128.0, -9.0)
CENTRES = (-43008.0, -42.0)
NY, NX, NZ = 96, 32, 128
PY = 104
PX = 104
WIDE = 4
PARTS = 8
CHUNK = 512 // PARTS


def band_matrix(size, centre):
    band = centre * np.eye(size, dtype=np.float32)
    for offset in range(1, 5):
        band += WEIGHTS[offset] * (np.eye(size, k=offset) + np.eye(size, k=-offset))
    return band


def band_pair():
    deep, wide = band_matrix(NZ, CENTRES[0]), band_matrix(NY, CENTRES[1])
    deep = np.kron(np.eye(2, dtype=np.float32), deep)
    return (jnp.asarray(np.concatenate([deep, deep], axis=0), jnp.bfloat16),
            jnp.asarray(np.concatenate([wide, wide], axis=1), jnp.bfloat16))


def position():
    s = lax.axis_index("shot")
    t = lax.axis_index("tile")
    return s // 8, (s // 2) % 4, s % 2, t // 2, t % 2


def device(xh, y, core, z, xl):
    return (xh * 8 + y * 2 + core, z * 2 + xl)


def meet(xh, y, core, z, xl, more, wanted, between):
    barrier = pltpu.get_barrier_semaphore()
    peers = []
    for a in range(2):
        for b in range(2):
            for e in range(2):
                if a or b or e:
                    peers.append(device((xh + a) % 2, y, (core + b) % 2, z, (xl + e) % 2))
    for d in range(1, 4):
        peers.append(device(xh, (y + d) % 4, core, z, xl))
    for peer in peers:
        pl.semaphore_signal(barrier, inc=1, device_id=peer, device_id_type=MESH_ID)
    @pl.when(wanted)
    def _():
        pl.semaphore_signal(barrier, inc=1, device_id=more, device_id_type=MESH_ID)
    between()
    pl.semaphore_wait(barrier, len(peers) + wanted.astype(jnp.int32))


def wave_kernel(blocks, wavelet, cell_in, depth_in, courant, damping, fwd, adj, records_in, band_z, band_y, out, *scratch):
    fields = (scratch[0:6], scratch[6:12])
    Z = scratch[12:14]
    (A, C, E, T, image, raw_f, raw_a, extra_in, extra, line, packed, ring, turned, lined, ssem, rsem,
     xsend, xrecv, fsend, ysend, yrecv, msend, mrecv, local, isend, irecv, osend, orecv) = scratch[14:]
    xh, y, core, z, xl = position()
    place = 2 * z + core
    has_left = place > 0
    has_right = place < 7
    left = device(xh, y, 1 - core, z - 1 + core, xl)
    right = device(xh, y, 1 - core, z + core, xl)
    beyond = device(xh, y, 1 - core, z - 1 + 2 * core, xl)
    lane = lax.broadcasted_iota(jnp.int32, (8, NZ), 1)
    row = lax.broadcasted_iota(jnp.int32, (8, NZ), 0)

    def pack():
        for h in range(2):
            extra_in[pl.ds(NY * h, NY), :] = records_in[pl.ds(4 * h, 4)].reshape(4 * NX, NY).T
        misc = jnp.zeros((8, NZ), jnp.float32)
        for m in range(8):
            misc = jnp.where(lane == m, wavelet[0, m], misc)
        misc = jnp.where(lane == 8, cell_in[0].astype(jnp.float32), misc)
        extra_in[pl.ds(2 * NY, 8), :] = jnp.where(lane == 9, depth_in[0].astype(jnp.float32), misc)

    meet(xh, y, core, z, xl, beyond, (z - 1 + 2 * core >= 0) & (z - 1 + 2 * core < 4), pack)
    away = core != xl
    home = core == xl

    def remote(source, target, send, recv, peer):
        return pltpu.make_async_remote_copy(src_ref=source, dst_ref=target, send_sem=send, recv_sem=recv,
                                            device_id=peer, device_id_type=MESH_ID)

    model = (courant, damping)

    def own(k, peer):
        return [remote(model[a], line.at[xh, core, a], xsend.at[k, a], xrecv.at[xh, core, a], peer) for a in range(2)]

    cross = own(0, device(1 - xh, y, xl, z, 1 - xl))
    pair = own(1, device(xh, y, xl, z, 1 - xl))
    inside = own(2, device(xh, y, 1 - core, z, xl))
    keep = [pltpu.make_async_copy(model[a], line.at[xh, core, a], local.at[a]) for a in range(2)]
    for a in range(2):
        pair[a].start()
        cross[a].start()
        pl.when(away)(inside[a].start)
        pl.when(home)(keep[a].start)

    partner = device(xh, y, xl, z, core)
    moves = []
    for k, (source, target) in enumerate(((extra_in, extra), (fwd, raw_f), (adj.at[0], raw_a.at[0]), (adj.at[1], raw_a.at[1]))):
        moves.append((remote(source, target, msend.at[k], mrecv.at[k], partner),
                      pltpu.make_async_copy(source, target, local.at[2 + k])))
    for far, near in moves:
        pl.when(away)(far.start)
        pl.when(home)(near.start)

    def arrived(a, b):
        for e in range(2):
            remote(line.at[a, b, e], line.at[a, b, e], xsend.at[0, e], xrecv.at[a, b, e], partner).wait_recv()

    def forward(b):
        return [remote(line.at[xh, b, a], line.at[xh, b, a], fsend.at[b, a], xrecv.at[xh, b, a],
                       device(1 - xh, y, core, z, 1 - xl)) for a in range(2)]

    @pl.when(away)
    def _():
        for b in range(2):
            arrived(xh, b)
            for copy in forward(b):
                copy.start()

    @pl.when(home)
    def _():
        for copy in keep:
            copy.wait()
        arrived(xh, 1 - core)

    for b in range(2):
        arrived(1 - xh, b)

    def pick(target, d):
        first = blocks[xh * 8 + ((y + d) % 4) * 2 + xl]
        for b in range(2):
            half = (2 * y + b < first).astype(jnp.int32)

            def rows(i, carry):
                part = pl.ds(pl.multiple_of(64 * i, 64), 64)
                target[b, :, part, :] = line[half, b, :, part, :]
                return carry
            lax.fori_loop(0, 8, rows, 0)

    def round_trip(d):
        return remote(packed.at[d - 1], ring.at[d], ysend.at[d - 1], yrecv.at[d - 1],
                      device(xh, (y + d) % 4, core, z, xl))

    for d in (2, 1, 3):
        pick(packed.at[d - 1], d)
        round_trip(d).start()
    def landed(i):
        far, near = moves[i]
        pl.when(away)(far.wait_recv)
        pl.when(home)(near.wait)

    def halo(f, slot, par, side):
        if side == 0:
            return pltpu.make_async_remote_copy(
                src_ref=fields[f][slot].at[pl.ds(4, 4), pl.ds(0, NY), :],
                dst_ref=fields[f][slot].at[pl.ds(36, 4), pl.ds(0, NY), :],
                send_sem=ssem.at[f, 0, par], recv_sem=rsem.at[f, 0, par],
                device_id=left, device_id_type=MESH_ID)
        return pltpu.make_async_remote_copy(
            src_ref=fields[f][slot].at[pl.ds(32, 4), pl.ds(0, NY), :],
            dst_ref=fields[f][slot].at[pl.ds(0, 4), pl.ds(0, NY), :],
            send_sem=ssem.at[f, 1, par], recv_sem=rsem.at[f, 1, par],
            device_id=right, device_id_type=MESH_ID)

    def send(f, slot, par, side):
        @pl.when(has_left if side == 0 else has_right)
        def _():
            halo(f, slot, par, side).start()

    def wait(f, slot, par):
        @pl.when(has_left)
        def _():
            halo(f, slot, par, 0).wait_send()
            halo(f, slot, par, 1).wait_recv()

        @pl.when(has_right)
        def _():
            halo(f, slot, par, 1).wait_send()
            halo(f, slot, par, 0).wait_recv()

    zero_side = jnp.zeros((4, NY, NZ), jnp.float32)

    @pl.when(place == 0)
    def _():
        for f in range(2):
            for slot in range(6):
                fields[f][slot][pl.ds(0, 4), pl.ds(0, NY), :] = zero_side

    @pl.when(place == 7)
    def _():
        for f in range(2):
            for slot in range(6):
                fields[f][slot][pl.ds(36, 4), pl.ds(0, NY), :] = zero_side

    landed(0)
    depth = jnp.broadcast_to(extra[pl.ds(192, 8), pl.ds(9, 1)], (8, NZ))
    plane = jnp.where(lane.astype(jnp.float32) == depth, 0.5, 0.0)
    cell = jnp.broadcast_to(extra[pl.ds(192, 8), pl.ds(8, 1)], (8, NZ))
    turns = [(depth + m) - jnp.where(depth + m >= NZ, float(NZ), 0.0) for m in range(8)]

    def load_extra(j, carry):
        rows = pl.ds(pl.multiple_of(8 * j, 8), 8)
        records = [extra[pl.ds(pl.multiple_of(NY * h + 8 * j, 8), 8), :] for h in range(2)]
        for x in range(NX):
            placed = jnp.zeros((8, NZ), jnp.float32)
            for m in range(8):
                at = (m % 4) * NX + x
                value = jnp.broadcast_to(records[m // 4][:, at:at + 1], (8, NZ))
                placed = jnp.where(lane.astype(jnp.float32) == turns[m], value, placed)
            T[x, rows, :] = placed
            index = (place * NX + x) * (NY * NZ) + (row + 8 * j) * NZ + lane
            E[x, rows, :] = jnp.where(index.astype(jnp.float32) == cell, 0.5, 0.0)
        return carry

    lax.fori_loop(0, NY // 8, load_extra, 0)

    def clear(x, carry):
        image[x] = jnp.zeros((6, 16, NZ), jnp.float32)
        return carry

    lax.fori_loop(0, NX, clear, 0)

    def load_state(f, slot, source):
        def planes(picks):
            def tiles(j, carry):
                rows = pl.ds(pl.multiple_of(8 * j, 8), 8)
                for x in picks:
                    fields[f][slot][4 + x, rows, :] = source[pl.ds(8 * NX * j + x, 8, stride=NX), :]
                return carry
            lax.fori_loop(0, NY // 8, tiles, 0)

        planes([*range(4), *range(28, 32)])
        if slot == 1:
            send(f, 1, 0, 0)
            send(f, 1, 0, 1)
        planes(range(4, 28))

    first = blocks[xh * 8 + y * 2 + xl]

    def choose(first, row, b):
        half = (2 * row + b < first).astype(jnp.int32)
        step = 8 * half + 2 * row + b - first
        inside = (step >= 0).astype(jnp.int32) * (step < 6).astype(jnp.int32)
        return half + 2 * (1 - inside), step

    def packet(d, q):
        return raw_f.at[0, pl.ds(2 * CHUNK * (3 * q + d - 1), 2 * CHUNK), :]

    def total_of(k, q):
        return raw_f.at[1, pl.ds(CHUNK * (4 * q + k), CHUNK), :]

    def turn(d, q):
        return remote(packet(d, q), turned.at[q, d], isend.at[q, d - 1], irecv.at[q, d - 1],
                      device(xh, (y + d) % 4, core, z, xl))

    def pick_image(target, d, q):
        for b in range(2):
            half, step = choose(first, (y + d) % 4, b)
            value = image[pl.ds(NX // PARTS * q, NX // PARTS), jnp.clip(step, 0, 5), :, :] * 0.125
            target[pl.ds(CHUNK * b, CHUNK), :] = value.reshape(CHUNK, NZ)

    def send_image(q):
        for d in (2, 1, 3):
            pick_image(packet(d, q), d, q)
            turn(d, q).start()
        pick_image(turned.at[q, 0], 0, q)

    def across(f, slot, x):
        for h in range(0, WIDE, 2):
            u = fields[f][slot][pl.ds(4 + x + h, 2), pl.ds(0, NY), :]
            high = u.astype(jnp.bfloat16)
            low = (u - high.astype(jnp.float32)).astype(jnp.bfloat16)
            high = jnp.concatenate([high[0], high[1]], axis=1)
            low = jnp.concatenate([low[0], low[1]], axis=1)
            rows = jnp.concatenate([high, low, band_y[...]], axis=1)
            columns = jnp.concatenate([band_z[...], high, low], axis=0)
            both = jnp.dot(rows, columns, preferred_element_type=jnp.float32)
            Z[f][x + h, pl.ds(0, NY), :] = both[:, :NZ]
            Z[f][x + h + 1, pl.ds(0, NY), :] = both[:, NZ:]

    def slot_of(n):
        return n + 1 if n < 5 else (n + 1) % 2

    def advance(f, n):
        cur, prev, new = fields[f][slot_of(n - 1)], fields[f][slot_of(n - 2)], fields[f][slot_of(n)]
        other = fields[1 - f][slot_of(9 - n)] if n > 4 else None
        wait(f, slot_of(n - 1), (n - 1) % 2)
        amp = jnp.broadcast_to(extra[pl.ds(192, 8), pl.ds(n - 1, 1)], (8, NZ))

        def planes(i, carry):
            x = WIDE * i
            if f == 0 and n > 1:
                across(1, slot_of(n - 1), x)
            if f == 1 and n < 8:
                across(0, slot_of(n), x)
            for j in range(NY // 8):
                rows = pl.ds(8 * j, 8)
                wide = cur[pl.ds(x, WIDE + 8), rows, :]
                u = wide[4:4 + WIDE]
                acc = Z[f][pl.ds(x, WIDE), rows, :]
                for k in range(1, 5):
                    acc = acc + WEIGHTS[k] * (wide[4 + k:4 + k + WIDE] + wide[4 - k:4 - k + WIDE])
                v = prev[pl.ds(4 + x, WIDE), rows, :]
                if f == 0:
                    force = E[pl.ds(x, WIDE), rows, :] * amp[None]
                else:
                    force = jnp.stack([pltpu.roll(T[x + h, rows, :], NZ - (8 - n), 1) * plane for h in range(WIDE)])
                w = v + A[pl.ds(x, WIDE), rows, :] * ((u - v) + (C[pl.ds(x, WIDE), rows, :] * acc + force))
                new[pl.ds(4 + x, WIDE), rows, :] = w
                if other is not None:
                    image[pl.ds(x, WIDE), j // 2, pl.ds(8 * (j % 2), 8), :] += w * other[pl.ds(4 + x, WIDE), rows, :]
            return carry

        if f == 1 and n == 8:
            for i in range(PARTS):
                planes(i, 0)
                send_image(i)
            return
        parts = [(0, 4 // WIDE, 0), (28 // WIDE, 32 // WIDE, 1), (4 // WIDE, 28 // WIDE, None)]
        for first, last, side in parts:
            lax.fori_loop(first, last, planes, 0)
            if side is not None and n < 8:
                send(f, slot_of(n), n % 2, side)

    def first_across(f):
        def planes(i, carry):
            across(f, 1, WIDE * i)
            return carry
        lax.fori_loop(0, NX // WIDE, planes, 0)

    landed(1)
    load_state(0, 1, raw_f.at[0])
    load_state(0, 0, raw_f.at[1])
    first_across(0)
    pick(ring.at[0], 0)
    for d in (1, 3, 2):
        round_trip(d).wait()


    def load_model(k, carry):
        j = first + k
        turn = (y - (j // 2) % 4 + 4) % 4
        parity = j % 2
        for h in range(2):
            rows = pl.ds(pl.multiple_of(16 * k + 8 * h, 8), 8)
            for x in range(NX):
                picked = pl.ds(8 * NX * h + x, 8, stride=NX)
                A[x, rows, :] = 2.0 / (1.0 + ring[turn, parity, 1, picked, :])
                C[x, rows, :] = ring[turn, parity, 0, picked, :] * (0.5 / SCALE)
        return carry

    lax.fori_loop(0, 6, load_model, 0)
    advance(0, 1)
    landed(2)
    load_state(1, 1, raw_a.at[0])
    first_across(1)
    landed(3)
    load_state(1, 0, raw_a.at[1])
    for n in range(1, 9):
        advance(1, n)
        if n < 8:
            advance(0, n + 1)

    def spread(k, q):
        return remote(total_of(k, q), lined.at[q, xh * 2 + xl], osend.at[q, k], orecv.at[q, xh * 2 + xl],
                      device(k // 2, y, k % 2, z, core))

    def mine(k):
        return (xh == k // 2) & (core == k % 2) & (xl == core)

    for q in range(PARTS):
        for d in (1, 3, 2):
            turn(d, q).wait_recv()
        for k in range(4):
            a, b = k // 2, k % 2
            total = jnp.zeros((CHUNK, NZ), jnp.float32)
            for d in range(4):
                half, step = choose(blocks[xh * 8 + ((y - d + 4) % 4) * 2 + xl], y, b)
                part = turned[q, d, pl.ds(CHUNK * b, CHUNK), :]
                total = total + jnp.where(jnp.full((CHUNK, NZ), half, jnp.int32) == a, part, 0.0)
            total_of(k, q)[...] = total

            @pl.when(jnp.logical_not(mine(k)))
            def _():
                spread(k, q).start()

            @pl.when(mine(k))
            def _():
                lined[q, xh * 2 + xl] = total_of(k, q)[...]

    for q in range(PARTS):
        for k in range(4):
            @pl.when(jnp.logical_not((xh * 2 + xl == k) & (xl == core)))
            def _():
                remote(lined.at[q, k], lined.at[q, k], osend.at[q, k], orecv.at[q, k],
                       device(k // 2, y, xl, z, k % 2)).wait_recv()
        total = (lined[q, 0] + lined[q, 1]) + (lined[q, 2] + lined[q, 3])
        for i in range(NX // PARTS):
            for h in range(2):
                out[pl.ds(8 * NX * h + NX // PARTS * q + i, 8, stride=NX), :] = total[16 * i + 8 * h:16 * i + 8 * h + 8]

    for q in range(PARTS):
        for d in (1, 3, 2):
            turn(d, q).wait_send()
        for k in range(4):
            @pl.when(jnp.logical_not(mine(k)))
            def _():
                spread(k, q).wait_send()

    for copy in pair + cross:
        copy.wait_send()

    @pl.when(away)
    def _():
        for copy in inside + forward(0) + forward(1):
            copy.wait_send()
        for far, near in moves:
            far.wait_send()


def run_wave(blocks, wavelet, cell, depth, courant, damping, fwd, adj, records):
    vm = pl.BlockSpec(memory_space=pltpu.VMEM)
    scalars = pl.BlockSpec(memory_space=pltpu.SMEM)
    anywhere = pl.BlockSpec(memory_space=pl.ANY)
    dma = pltpu.SemaphoreType.DMA
    full = lambda: pltpu.VMEM((NX, PX, NZ), jnp.float32)
    flat = lambda *shape: pltpu.VMEM((*shape, NZ), jnp.float32)
    return pl.pallas_call(
        wave_kernel,
        out_shape=jax.ShapeDtypeStruct((512, NZ), jnp.float32),
        in_specs=[scalars] * 4 + [anywhere] * 4 + [vm] * 3,
        out_specs=vm,
        scratch_shapes=[
            *[flat(NX + 8, PY) for _ in range(12)],
            *[full() for _ in range(6)],
            flat(NX, 6, 16),
            flat(2, NY * NX),
            flat(2, NY * NX),
            flat(2 * NY + 8),
            flat(2 * NY + 8),
            flat(2, 2, 2, 512),
            flat(3, 2, 2, 512),
            flat(4, 2, 2, 512),
            flat(PARTS, 4, 2 * CHUNK),
            flat(PARTS, 4, CHUNK),
            dma((2, 2, 2)), dma((2, 2, 2)),
            dma((3, 2)), dma((2, 2, 2)), dma((2, 2)), dma((3,)), dma((3,)), dma((4,)), dma((4,)), dma((6,)),
            dma((PARTS, 3)), dma((PARTS, 3)), dma((PARTS, 4)), dma((PARTS, 4)),
        ],
        compiler_params=pltpu.CompilerParams(collective_id=1, has_side_effects=True, vmem_limit_bytes=61 << 20),
        name="wave_steps",
    )(blocks, wavelet, cell, depth, courant, damping, fwd, adj, records, *band_pair())


def body(courant, damping, aperture_block, source_cell, receiver_depth, wavelet, receiver_data,
         forward_state, adjoint_state):
    image = run_wave(aperture_block, wavelet, source_cell, receiver_depth, courant.reshape(512, NZ),
                     damping.reshape(512, NZ), forward_state[0].reshape(2, NY * NX, NZ),
                     adjoint_state[0].reshape(2, NY * NX, NZ), receiver_data[0].transpose(0, 2, 1))
    return image.reshape(16, NX, NZ)


def solution(mesh):
    placed = (
        P("shot", "tile", None),
        P("shot", "tile", None),
        P(),
        P("shot"),
        P("shot"),
        P("shot", None),
        P("shot", None, None, "tile"),
        P("shot", None, None, "tile", None),
        P("shot", None, None, "tile", None),
    )
    return jax.shard_map(
        body, mesh=mesh, in_specs=placed, out_specs=P("shot", "tile", None), check_vma=False
    )
```

```python
import functools
import jax
import jax.numpy as jnp
import numpy as np
from jax import lax
from jax.experimental import pallas as pl
from jax.experimental.pallas import tpu as pltpu
from jax.sharding import PartitionSpec as P

MESH_ID = pl.DeviceIdType.MESH
SCALE = 5040.0
WEIGHTS = (-43050.0, 8064.0, -1008.0, 128.0, -9.0)
CENTRES = (-43008.0, -42.0)
NY, NX, NZ = 96, 32, 128
PY = 104
PX = 104
WIDE = 4
PARTS = 8
CHUNK = 512 // PARTS


def band_matrix(size, centre):
    band = centre * np.eye(size, dtype=np.float32)
    for offset in range(1, 5):
        band += WEIGHTS[offset] * (np.eye(size, k=offset) + np.eye(size, k=-offset))
    return band


def band_pair():
    deep, wide = band_matrix(NZ, CENTRES[0]), band_matrix(NY, CENTRES[1])
    deep = np.kron(np.eye(2, dtype=np.float32), deep)
    return (jnp.asarray(np.concatenate([deep, deep], axis=0), jnp.bfloat16),
            jnp.asarray(np.concatenate([wide, wide], axis=1), jnp.bfloat16))


def position():
    s = lax.axis_index("shot")
    t = lax.axis_index("tile")
    return s // 8, (s // 2) % 4, s % 2, t // 2, t % 2


def device(xh, y, core, z, xl):
    return (xh * 8 + y * 2 + core, z * 2 + xl)


def meet(xh, y, core, z, xl, more, wanted, between):
    barrier = pltpu.get_barrier_semaphore()
    peers = []
    for a in range(2):
        for b in range(2):
            for e in range(2):
                if a or b or e:
                    peers.append(device((xh + a) % 2, y, (core + b) % 2, z, (xl + e) % 2))
    for d in range(1, 4):
        peers.append(device(xh, (y + d) % 4, core, z, xl))
    for peer in peers:
        pl.semaphore_signal(barrier, inc=1, device_id=peer, device_id_type=MESH_ID)
    @pl.when(wanted)
    def _():
        pl.semaphore_signal(barrier, inc=1, device_id=more, device_id_type=MESH_ID)
    between()
    pl.semaphore_wait(barrier, len(peers) + wanted.astype(jnp.int32))


def wave_kernel(blocks, wavelet, cell_in, depth_in, courant, damping, fwd, adj, records_in, band_z, band_y, out, *scratch):
    fields = (scratch[0:6], scratch[6:12])
    Z = scratch[12:14]
    (A, C, E, T, image, raw_f, raw_a, extra_in, extra, line, packed, ring, turned, lined, ssem, rsem,
     xsend, xrecv, fsend, ysend, yrecv, msend, mrecv, local, isend, irecv, osend, orecv, xfirst, ysecond,
     csend, crecv, dsend, drecv) = scratch[14:]
    xh, y, core, z, xl = position()
    place = 2 * z + core
    has_left = place > 0
    has_right = place < 7
    left = device(xh, y, 1 - core, z - 1 + core, xl)
    right = device(xh, y, 1 - core, z + core, xl)
    beyond = device(xh, y, 1 - core, z - 1 + 2 * core, xl)
    lane = lax.broadcasted_iota(jnp.int32, (8, NZ), 1)
    row = lax.broadcasted_iota(jnp.int32, (8, NZ), 0)

    def pack():
        for h in range(2):
            extra_in[pl.ds(NY * h, NY), :] = records_in[pl.ds(4 * h, 4)].reshape(4 * NX, NY).T
        misc = jnp.zeros((8, NZ), jnp.float32)
        for m in range(8):
            misc = jnp.where(lane == m, wavelet[0, m], misc)
        misc = jnp.where(lane == 8, cell_in[0].astype(jnp.float32), misc)
        extra_in[pl.ds(2 * NY, 8), :] = jnp.where(lane == 9, depth_in[0].astype(jnp.float32), misc)

    meet(xh, y, core, z, xl, beyond, (z - 1 + 2 * core >= 0) & (z - 1 + 2 * core < 4), pack)
    away = core != xl
    home = core == xl

    def remote(source, target, send, recv, peer):
        return pltpu.make_async_remote_copy(src_ref=source, dst_ref=target, send_sem=send, recv_sem=recv,
                                            device_id=peer, device_id_type=MESH_ID)

    model = (courant, damping)

    def own(k, peer):
        return [remote(model[a], line.at[xh, core, a], xsend.at[k, a], xrecv.at[xh, core, a], peer) for a in range(2)]

    cross = own(0, device(1 - xh, y, xl, z, 1 - xl))
    pair = own(1, device(xh, y, xl, z, 1 - xl))
    inside = own(2, device(xh, y, 1 - core, z, xl))
    keep = [pltpu.make_async_copy(model[a], line.at[xh, core, a], local.at[a]) for a in range(2)]
    for a in range(2):
        pair[a].start()
        cross[a].start()
        pl.when(away)(inside[a].start)
        pl.when(home)(keep[a].start)

    partner = device(xh, y, xl, z, core)
    moves = []
    for k, (source, target) in enumerate(((extra_in, extra), (fwd, raw_f), (adj.at[0], raw_a.at[0]), (adj.at[1], raw_a.at[1]))):
        moves.append((remote(source, target, msend.at[k], mrecv.at[k], partner),
                      pltpu.make_async_copy(source, target, local.at[2 + k])))
    for far, near in moves:
        pl.when(away)(far.start)
        pl.when(home)(near.start)

    def arrived(a, b):
        for e in range(2):
            remote(line.at[a, b, e], line.at[a, b, e], xsend.at[0, e], xrecv.at[a, b, e], partner).wait_recv()

    def forward(b):
        return [remote(line.at[xh, b, a], line.at[xh, b, a], fsend.at[b, a], xrecv.at[xh, b, a],
                       device(1 - xh, y, core, z, 1 - xl)) for a in range(2)]

    @pl.when(away)
    def _():
        for b in range(2):
            arrived(xh, b)
            for copy in forward(b):
                copy.start()

    @pl.when(home)
    def _():
        for copy in keep:
            copy.wait()
        arrived(xh, 1 - core)

    for b in range(2):
        arrived(1 - xh, b)

    def pick(target, d):
        first = blocks[xh * 8 + ((y + d) % 4) * 2 + xl]
        for b in range(2):
            half = (2 * y + b < first).astype(jnp.int32)

            def rows(i, carry):
                part = pl.ds(pl.multiple_of(64 * i, 64), 64)
                target[b, :, part, :] = line[half, b, :, part, :]
                return carry
            lax.fori_loop(0, 8, rows, 0)

    def round_trip(d):
        return remote(packed.at[d - 1], ring.at[d], ysend.at[d - 1], yrecv.at[d - 1],
                      device(xh, (y + d) % 4, core, z, xl))

    for d in (2, 1, 3):
        pick(packed.at[d - 1], d)
        round_trip(d).start()
    def landed(i):
        far, near = moves[i]
        pl.when(away)(far.wait_recv)
        pl.when(home)(near.wait)

    def halo(f, slot, par, side):
        if side == 0:
            return pltpu.make_async_remote_copy(
                src_ref=fields[f][slot].at[pl.ds(4, 4), pl.ds(0, NY), :],
                dst_ref=fields[f][slot].at[pl.ds(36, 4), pl.ds(0, NY), :],
                send_sem=ssem.at[f, 0, par], recv_sem=rsem.at[f, 0, par],
                device_id=left, device_id_type=MESH_ID)
        return pltpu.make_async_remote_copy(
            src_ref=fields[f][slot].at[pl.ds(32, 4), pl.ds(0, NY), :],
            dst_ref=fields[f][slot].at[pl.ds(0, 4), pl.ds(0, NY), :],
            send_sem=ssem.at[f, 1, par], recv_sem=rsem.at[f, 1, par],
            device_id=right, device_id_type=MESH_ID)

    def send(f, slot, par, side):
        @pl.when(has_left if side == 0 else has_right)
        def _():
            halo(f, slot, par, side).start()

    def wait(f, slot, par):
        @pl.when(has_left)
        def _():
            halo(f, slot, par, 0).wait_send()
            halo(f, slot, par, 1).wait_recv()

        @pl.when(has_right)
        def _():
            halo(f, slot, par, 1).wait_send()
            halo(f, slot, par, 0).wait_recv()

    zero_side = jnp.zeros((4, NY, NZ), jnp.float32)

    @pl.when(place == 0)
    def _():
        for f in range(2):
            for slot in range(6):
                fields[f][slot][pl.ds(0, 4), pl.ds(0, NY), :] = zero_side

    @pl.when(place == 7)
    def _():
        for f in range(2):
            for slot in range(6):
                fields[f][slot][pl.ds(36, 4), pl.ds(0, NY), :] = zero_side

    landed(0)
    depth = jnp.broadcast_to(extra[pl.ds(192, 8), pl.ds(9, 1)], (8, NZ))
    plane = jnp.where(lane.astype(jnp.float32) == depth, 0.5, 0.0)
    cell = jnp.broadcast_to(extra[pl.ds(192, 8), pl.ds(8, 1)], (8, NZ))
    turns = [(depth + m) - jnp.where(depth + m >= NZ, float(NZ), 0.0) for m in range(8)]

    def load_extra(j, carry):
        rows = pl.ds(pl.multiple_of(8 * j, 8), 8)
        records = [extra[pl.ds(pl.multiple_of(NY * h + 8 * j, 8), 8), :] for h in range(2)]
        for x in range(NX):
            placed = jnp.zeros((8, NZ), jnp.float32)
            for m in range(8):
                at = (m % 4) * NX + x
                value = jnp.broadcast_to(records[m // 4][:, at:at + 1], (8, NZ))
                placed = jnp.where(lane.astype(jnp.float32) == turns[m], value, placed)
            T[x, rows, :] = placed
            index = (place * NX + x) * (NY * NZ) + (row + 8 * j) * NZ + lane
            E[x, rows, :] = jnp.where(index.astype(jnp.float32) == cell, 0.5, 0.0)
        return carry

    lax.fori_loop(0, NY // 8, load_extra, 0)

    def clear(x, carry):
        image[x] = jnp.zeros((6, 16, NZ), jnp.float32)
        return carry

    lax.fori_loop(0, NX, clear, 0)

    def load_state(f, slot, source):
        def planes(picks):
            def tiles(j, carry):
                rows = pl.ds(pl.multiple_of(8 * j, 8), 8)
                for x in picks:
                    fields[f][slot][4 + x, rows, :] = source[pl.ds(8 * NX * j + x, 8, stride=NX), :]
                return carry
            lax.fori_loop(0, NY // 8, tiles, 0)

        planes([*range(4), *range(28, 32)])
        if slot == 1:
            send(f, 1, 0, 0)
            send(f, 1, 0, 1)
        planes(range(4, 28))

    first = blocks[xh * 8 + y * 2 + xl]

    def choose(first, row, b):
        half = (2 * row + b < first).astype(jnp.int32)
        step = 8 * half + 2 * row + b - first
        inside = (step >= 0).astype(jnp.int32) * (step < 6).astype(jnp.int32)
        return half + 2 * (1 - inside), step

    def packet(d, q):
        return raw_f.at[0, pl.ds(2 * CHUNK * (3 * q + d - 1), 2 * CHUNK), :]

    def total_of(k, q):
        return raw_f.at[1, pl.ds(CHUNK * (4 * q + k), CHUNK), :]

    def turn(d, q):
        return remote(packet(d, q), turned.at[q, d], isend.at[q, d - 1], irecv.at[q, d - 1],
                      device(xh, (y + d) % 4, core, z, xl))

    def pick_image(target, d, q):
        for b in range(2):
            half, step = choose(first, (y + d) % 4, b)
            value = image[pl.ds(NX // PARTS * q, NX // PARTS), jnp.clip(step, 0, 5), :, :] * 0.125
            target[pl.ds(CHUNK * b, CHUNK), :] = value.reshape(CHUNK, NZ)

    def send_image(q):
        for d in (2, 1, 3):
            pick_image(packet(d, q), d, q)
            turn(d, q).start()
        pick_image(turned.at[q, 0], 0, q)

    def mine(k):
        return (xh == k // 2) & (core == k % 2) & (xl == core)

    def line_copy(k):
        return remote(raw_a.at[0, pl.ds(4 * CHUNK * k, 4 * CHUNK), :], xfirst.at[xh * 2 + xl], csend.at[k],
                      crecv.at[xh * 2 + xl], device(k // 2, y, k % 2, z, core))

    def send_first():
        for k in range(4):
            for r in range(4):
                step = 8 * (k // 2) + 2 * r + k % 2 - first
                inside = (step >= 0).astype(jnp.int32) * (step < 6).astype(jnp.int32)
                value = image[pl.ds(0, NX // PARTS), jnp.clip(step, 0, 5), :, :] * 0.125
                kept = jnp.full((CHUNK, NZ), inside, jnp.int32) == 1
                raw_a[0, pl.ds(CHUNK * (4 * k + r), CHUNK), :] = jnp.where(kept, value.reshape(CHUNK, NZ), 0.0)

            @pl.when(jnp.logical_not(mine(k)))
            def _():
                line_copy(k).start()

            @pl.when(mine(k))
            def _():
                xfirst[xh * 2 + xl] = raw_a[0, pl.ds(4 * CHUNK * k, 4 * CHUNK), :]

    def column_copy(d):
        row = (y + d) % 4
        return remote(raw_a.at[1, pl.ds(pl.multiple_of(CHUNK * row, CHUNK), CHUNK), :], ysecond.at[d], dsend.at[d - 1],
                      drecv.at[d - 1], device(xh, row, core, z, xl))

    def across(f, slot, x):
        for h in range(0, WIDE, 2):
            u = fields[f][slot][pl.ds(4 + x + h, 2), pl.ds(0, NY), :]
            high = u.astype(jnp.bfloat16)
            low = (u - high.astype(jnp.float32)).astype(jnp.bfloat16)
            high = jnp.concatenate([high[0], high[1]], axis=1)
            low = jnp.concatenate([low[0], low[1]], axis=1)
            rows = jnp.concatenate([high, low, band_y[...]], axis=1)
            columns = jnp.concatenate([band_z[...], high, low], axis=0)
            both = jnp.dot(rows, columns, preferred_element_type=jnp.float32)
            Z[f][x + h, pl.ds(0, NY), :] = both[:, :NZ]
            Z[f][x + h + 1, pl.ds(0, NY), :] = both[:, NZ:]

    def slot_of(n):
        return n + 1 if n < 5 else (n + 1) % 2

    def advance(f, n):
        cur, prev, new = fields[f][slot_of(n - 1)], fields[f][slot_of(n - 2)], fields[f][slot_of(n)]
        other = fields[1 - f][slot_of(9 - n)] if n > 4 else None
        wait(f, slot_of(n - 1), (n - 1) % 2)
        amp = jnp.broadcast_to(extra[pl.ds(192, 8), pl.ds(n - 1, 1)], (8, NZ))

        def planes(i, carry):
            x = WIDE * i
            if f == 0 and n > 1:
                across(1, slot_of(n - 1), x)
            if f == 1 and n < 8:
                across(0, slot_of(n), x)
            for j in range(NY // 8):
                rows = pl.ds(8 * j, 8)
                wide = cur[pl.ds(x, WIDE + 8), rows, :]
                u = wide[4:4 + WIDE]
                acc = Z[f][pl.ds(x, WIDE), rows, :]
                for k in range(1, 5):
                    acc = acc + WEIGHTS[k] * (wide[4 + k:4 + k + WIDE] + wide[4 - k:4 - k + WIDE])
                v = prev[pl.ds(4 + x, WIDE), rows, :]
                if f == 0:
                    force = E[pl.ds(x, WIDE), rows, :] * amp[None]
                else:
                    force = jnp.stack([pltpu.roll(T[x + h, rows, :], NZ - (8 - n), 1) * plane for h in range(WIDE)])
                w = v + A[pl.ds(x, WIDE), rows, :] * ((u - v) + (C[pl.ds(x, WIDE), rows, :] * acc + force))
                new[pl.ds(4 + x, WIDE), rows, :] = w
                if other is not None:
                    image[pl.ds(x, WIDE), j // 2, pl.ds(8 * (j % 2), 8), :] += w * other[pl.ds(4 + x, WIDE), rows, :]
            return carry

        if f == 1 and n == 8:
            for i in range(PARTS):
                planes(i, 0)
                if i == 0:
                    send_first()
                else:
                    send_image(i)
            return
        parts = [(0, 4 // WIDE, 0), (28 // WIDE, 32 // WIDE, 1), (4 // WIDE, 28 // WIDE, None)]
        for first, last, side in parts:
            lax.fori_loop(first, last, planes, 0)
            if side is not None and n < 8:
                send(f, slot_of(n), n % 2, side)

    def first_across(f):
        def planes(i, carry):
            across(f, 1, WIDE * i)
            return carry
        lax.fori_loop(0, NX // WIDE, planes, 0)

    landed(1)
    load_state(0, 1, raw_f.at[0])
    load_state(0, 0, raw_f.at[1])
    first_across(0)
    pick(ring.at[0], 0)
    for d in (1, 3, 2):
        round_trip(d).wait()


    def load_model(k, carry):
        j = first + k
        turn = (y - (j // 2) % 4 + 4) % 4
        parity = j % 2
        for h in range(2):
            rows = pl.ds(pl.multiple_of(16 * k + 8 * h, 8), 8)
            for x in range(NX):
                picked = pl.ds(8 * NX * h + x, 8, stride=NX)
                A[x, rows, :] = 2.0 / (1.0 + ring[turn, parity, 1, picked, :])
                C[x, rows, :] = ring[turn, parity, 0, picked, :] * (0.5 / SCALE)
        return carry

    lax.fori_loop(0, 6, load_model, 0)
    advance(0, 1)
    landed(2)
    load_state(1, 1, raw_a.at[0])
    first_across(1)
    landed(3)
    load_state(1, 0, raw_a.at[1])
    for n in range(1, 9):
        advance(1, n)
        if n < 8:
            advance(0, n + 1)

    def spread(k, q):
        return remote(total_of(k, q), lined.at[q, xh * 2 + xl], osend.at[q, k], orecv.at[q, xh * 2 + xl],
                      device(k // 2, y, k % 2, z, core))

    for k in range(4):
        @pl.when(jnp.logical_not((xh * 2 + xl == k) & (xl == core)))
        def _():
            remote(xfirst.at[k], xfirst.at[k], csend.at[0], crecv.at[k], device(k // 2, y, xl, z, k % 2)).wait_recv()
    raw_a[1, pl.ds(0, 4 * CHUNK), :] = (xfirst[0] + xfirst[1]) + (xfirst[2] + xfirst[3])
    for d in (2, 1, 3):
        column_copy(d).start()
    ysecond[0] = raw_a[1, pl.ds(pl.multiple_of(CHUNK * y, CHUNK), CHUNK), :]

    for q in range(1, PARTS):
        for d in (1, 3, 2):
            turn(d, q).wait_recv()
        for k in range(4):
            a, b = k // 2, k % 2
            total = jnp.zeros((CHUNK, NZ), jnp.float32)
            for d in range(4):
                half, step = choose(blocks[xh * 8 + ((y - d + 4) % 4) * 2 + xl], y, b)
                part = turned[q, d, pl.ds(CHUNK * b, CHUNK), :]
                total = total + jnp.where(jnp.full((CHUNK, NZ), half, jnp.int32) == a, part, 0.0)
            total_of(k, q)[...] = total

            @pl.when(jnp.logical_not(mine(k)))
            def _():
                spread(k, q).start()

            @pl.when(mine(k))
            def _():
                lined[q, xh * 2 + xl] = total_of(k, q)[...]

    for q in range(PARTS):
        if q == 0:
            for d in (1, 3, 2):
                column_copy(d).wait_recv()
            total = (ysecond[0] + ysecond[1]) + (ysecond[2] + ysecond[3])
        else:
            for k in range(4):
                @pl.when(jnp.logical_not((xh * 2 + xl == k) & (xl == core)))
                def _():
                    remote(lined.at[q, k], lined.at[q, k], osend.at[q, k], orecv.at[q, k],
                           device(k // 2, y, xl, z, k % 2)).wait_recv()
            total = (lined[q, 0] + lined[q, 1]) + (lined[q, 2] + lined[q, 3])
        for i in range(NX // PARTS):
            for h in range(2):
                out[pl.ds(8 * NX * h + NX // PARTS * q + i, 8, stride=NX), :] = total[16 * i + 8 * h:16 * i + 8 * h + 8]

    for d in (1, 3, 2):
        column_copy(d).wait_send()
    for k in range(4):
        @pl.when(jnp.logical_not(mine(k)))
        def _():
            line_copy(k).wait_send()
    for q in range(1, PARTS):
        for d in (1, 3, 2):
            turn(d, q).wait_send()
        for k in range(4):
            @pl.when(jnp.logical_not(mine(k)))
            def _():
                spread(k, q).wait_send()

    for copy in pair + cross:
        copy.wait_send()

    @pl.when(away)
    def _():
        for copy in inside + forward(0) + forward(1):
            copy.wait_send()
        for far, near in moves:
            far.wait_send()


def run_wave(blocks, wavelet, cell, depth, courant, damping, fwd, adj, records):
    vm = pl.BlockSpec(memory_space=pltpu.VMEM)
    scalars = pl.BlockSpec(memory_space=pltpu.SMEM)
    anywhere = pl.BlockSpec(memory_space=pl.ANY)
    dma = pltpu.SemaphoreType.DMA
    full = lambda: pltpu.VMEM((NX, PX, NZ), jnp.float32)
    flat = lambda *shape: pltpu.VMEM((*shape, NZ), jnp.float32)
    return pl.pallas_call(
        wave_kernel,
        out_shape=jax.ShapeDtypeStruct((512, NZ), jnp.float32),
        in_specs=[scalars] * 4 + [anywhere] * 4 + [vm] * 3,
        out_specs=vm,
        scratch_shapes=[
            *[flat(NX + 8, PY) for _ in range(12)],
            *[full() for _ in range(6)],
            flat(NX, 6, 16),
            flat(2, NY * NX),
            flat(2, NY * NX),
            flat(2 * NY + 8),
            flat(2 * NY + 8),
            flat(2, 2, 2, 512),
            flat(3, 2, 2, 512),
            flat(4, 2, 2, 512),
            flat(PARTS, 4, 2 * CHUNK),
            flat(PARTS, 4, CHUNK),
            dma((2, 2, 2)), dma((2, 2, 2)),
            dma((3, 2)), dma((2, 2, 2)), dma((2, 2)), dma((3,)), dma((3,)), dma((4,)), dma((4,)), dma((6,)),
            dma((PARTS, 3)), dma((PARTS, 3)), dma((PARTS, 4)), dma((PARTS, 4)),
            flat(4, 4 * CHUNK),
            flat(4, CHUNK),
            dma((4,)), dma((4,)), dma((3,)), dma((3,)),
        ],
        compiler_params=pltpu.CompilerParams(collective_id=1, has_side_effects=True, vmem_limit_bytes=61 << 20),
        name="wave_steps",
    )(blocks, wavelet, cell, depth, courant, damping, fwd, adj, records, *band_pair())


def body(courant, damping, aperture_block, source_cell, receiver_depth, wavelet, receiver_data,
         forward_state, adjoint_state):
    image = run_wave(aperture_block, wavelet, source_cell, receiver_depth, courant.reshape(512, NZ),
                     damping.reshape(512, NZ), forward_state[0].reshape(2, NY * NX, NZ),
                     adjoint_state[0].reshape(2, NY * NX, NZ), receiver_data[0].transpose(0, 2, 1))
    return image.reshape(16, NX, NZ)


def solution(mesh):
    placed = (
        P("shot", "tile", None),
        P("shot", "tile", None),
        P(),
        P("shot"),
        P("shot"),
        P("shot", None),
        P("shot", None, None, "tile"),
        P("shot", None, None, "tile", None),
        P("shot", None, None, "tile", None),
    )
    return jax.shard_map(
        body, mesh=mesh, in_specs=placed, out_specs=P("shot", "tile", None), check_vma=False
    )
```

```python
import functools
import jax
import jax.numpy as jnp
import numpy as np
from jax import lax
from jax.experimental import pallas as pl
from jax.experimental.pallas import tpu as pltpu
from jax.sharding import PartitionSpec as P

MESH_ID = pl.DeviceIdType.MESH
SCALE = 5040.0
WEIGHTS = (-43050.0, 8064.0, -1008.0, 128.0, -9.0)
CENTRES = (-43008.0, -42.0)
NY, NX, NZ = 96, 32, 128
PY = 104
PX = 104
WIDE = 4
INNER = 8
PARTS = 8
CHUNK = 512 // PARTS


def band_matrix(size, centre):
    band = centre * np.eye(size, dtype=np.float32)
    for offset in range(1, 5):
        band += WEIGHTS[offset] * (np.eye(size, k=offset) + np.eye(size, k=-offset))
    return band


def band_pair():
    deep, wide = band_matrix(NZ, CENTRES[0]), band_matrix(NY, CENTRES[1])
    deep = np.kron(np.eye(2, dtype=np.float32), deep)
    return (jnp.asarray(np.concatenate([deep, deep], axis=0), jnp.bfloat16),
            jnp.asarray(np.concatenate([wide, wide], axis=1), jnp.bfloat16))


def position():
    s = lax.axis_index("shot")
    t = lax.axis_index("tile")
    return s // 8, (s // 2) % 4, s % 2, t // 2, t % 2


def device(xh, y, core, z, xl):
    return (xh * 8 + y * 2 + core, z * 2 + xl)


def meet(xh, y, core, z, xl, more, wanted, between):
    barrier = pltpu.get_barrier_semaphore()
    peers = []
    for a in range(2):
        for b in range(2):
            for e in range(2):
                if a or b or e:
                    peers.append(device((xh + a) % 2, y, (core + b) % 2, z, (xl + e) % 2))
    for d in range(1, 4):
        peers.append(device(xh, (y + d) % 4, core, z, xl))
    for peer in peers:
        pl.semaphore_signal(barrier, inc=1, device_id=peer, device_id_type=MESH_ID)
    @pl.when(wanted)
    def _():
        pl.semaphore_signal(barrier, inc=1, device_id=more, device_id_type=MESH_ID)
    between()
    pl.semaphore_wait(barrier, len(peers) + wanted.astype(jnp.int32))


def wave_kernel(blocks, wavelet, cell_in, depth_in, courant, damping, fwd, adj, records_in, band_z, band_y, out, *scratch):
    fields = (scratch[0:6], scratch[6:12])
    Z = scratch[12:14]
    (A, C, E, T, image, raw_f, raw_a, extra_in, extra, line, packed, ring, turned, lined, ssem, rsem,
     xsend, xrecv, fsend, ysend, yrecv, msend, mrecv, local, isend, irecv, osend, orecv, xfirst, ysecond,
     csend, crecv, dsend, drecv) = scratch[14:]
    xh, y, core, z, xl = position()
    place = 2 * z + core
    has_left = place > 0
    has_right = place < 7
    left = device(xh, y, 1 - core, z - 1 + core, xl)
    right = device(xh, y, 1 - core, z + core, xl)
    beyond = device(xh, y, 1 - core, z - 1 + 2 * core, xl)
    lane = lax.broadcasted_iota(jnp.int32, (8, NZ), 1)
    row = lax.broadcasted_iota(jnp.int32, (8, NZ), 0)

    def pack():
        for h in range(2):
            extra_in[pl.ds(NY * h, NY), :] = records_in[pl.ds(4 * h, 4)].reshape(4 * NX, NY).T
        misc = jnp.zeros((8, NZ), jnp.float32)
        for m in range(8):
            misc = jnp.where(lane == m, wavelet[0, m], misc)
        misc = jnp.where(lane == 8, cell_in[0].astype(jnp.float32), misc)
        extra_in[pl.ds(2 * NY, 8), :] = jnp.where(lane == 9, depth_in[0].astype(jnp.float32), misc)

    meet(xh, y, core, z, xl, beyond, (z - 1 + 2 * core >= 0) & (z - 1 + 2 * core < 4), pack)
    away = core != xl
    home = core == xl

    def remote(source, target, send, recv, peer):
        return pltpu.make_async_remote_copy(src_ref=source, dst_ref=target, send_sem=send, recv_sem=recv,
                                            device_id=peer, device_id_type=MESH_ID)

    model = (courant, damping)

    def own(k, peer):
        return [remote(model[a], line.at[xh, core, a], xsend.at[k, a], xrecv.at[xh, core, a], peer) for a in range(2)]

    cross = own(0, device(1 - xh, y, xl, z, 1 - xl))
    pair = own(1, device(xh, y, xl, z, 1 - xl))
    inside = own(2, device(xh, y, 1 - core, z, xl))
    keep = [pltpu.make_async_copy(model[a], line.at[xh, core, a], local.at[a]) for a in range(2)]
    for a in range(2):
        pair[a].start()
        cross[a].start()
        pl.when(away)(inside[a].start)
        pl.when(home)(keep[a].start)

    partner = device(xh, y, xl, z, core)
    moves = []
    for k, (source, target) in enumerate(((extra_in, extra), (fwd, raw_f), (adj.at[0], raw_a.at[0]), (adj.at[1], raw_a.at[1]))):
        moves.append((remote(source, target, msend.at[k], mrecv.at[k], partner),
                      pltpu.make_async_copy(source, target, local.at[2 + k])))
    for far, near in moves:
        pl.when(away)(far.start)
        pl.when(home)(near.start)

    def arrived(a, b):
        for e in range(2):
            remote(line.at[a, b, e], line.at[a, b, e], xsend.at[0, e], xrecv.at[a, b, e], partner).wait_recv()

    def forward(b):
        return [remote(line.at[xh, b, a], line.at[xh, b, a], fsend.at[b, a], xrecv.at[xh, b, a],
                       device(1 - xh, y, core, z, 1 - xl)) for a in range(2)]

    @pl.when(away)
    def _():
        for b in range(2):
            arrived(xh, b)
            for copy in forward(b):
                copy.start()

    @pl.when(home)
    def _():
        for copy in keep:
            copy.wait()
        arrived(xh, 1 - core)

    for b in range(2):
        arrived(1 - xh, b)

    def pick(target, d):
        first = blocks[xh * 8 + ((y + d) % 4) * 2 + xl]
        for b in range(2):
            half = (2 * y + b < first).astype(jnp.int32)

            def rows(i, carry):
                part = pl.ds(pl.multiple_of(64 * i, 64), 64)
                target[b, :, part, :] = line[half, b, :, part, :]
                return carry
            lax.fori_loop(0, 8, rows, 0)

    def round_trip(d):
        return remote(packed.at[d - 1], ring.at[d], ysend.at[d - 1], yrecv.at[d - 1],
                      device(xh, (y + d) % 4, core, z, xl))

    for d in (2, 1, 3):
        pick(packed.at[d - 1], d)
        round_trip(d).start()
    def landed(i):
        far, near = moves[i]
        pl.when(away)(far.wait_recv)
        pl.when(home)(near.wait)

    def halo(f, slot, par, side):
        if side == 0:
            return pltpu.make_async_remote_copy(
                src_ref=fields[f][slot].at[pl.ds(4, 4), pl.ds(0, NY), :],
                dst_ref=fields[f][slot].at[pl.ds(36, 4), pl.ds(0, NY), :],
                send_sem=ssem.at[f, 0, par], recv_sem=rsem.at[f, 0, par],
                device_id=left, device_id_type=MESH_ID)
        return pltpu.make_async_remote_copy(
            src_ref=fields[f][slot].at[pl.ds(32, 4), pl.ds(0, NY), :],
            dst_ref=fields[f][slot].at[pl.ds(0, 4), pl.ds(0, NY), :],
            send_sem=ssem.at[f, 1, par], recv_sem=rsem.at[f, 1, par],
            device_id=right, device_id_type=MESH_ID)

    def send(f, slot, par, side):
        @pl.when(has_left if side == 0 else has_right)
        def _():
            halo(f, slot, par, side).start()

    def wait(f, slot, par):
        @pl.when(has_left)
        def _():
            halo(f, slot, par, 0).wait_send()
            halo(f, slot, par, 1).wait_recv()

        @pl.when(has_right)
        def _():
            halo(f, slot, par, 1).wait_send()
            halo(f, slot, par, 0).wait_recv()

    zero_side = jnp.zeros((4, NY, NZ), jnp.float32)

    @pl.when(place == 0)
    def _():
        for f in range(2):
            for slot in range(6):
                fields[f][slot][pl.ds(0, 4), pl.ds(0, NY), :] = zero_side

    @pl.when(place == 7)
    def _():
        for f in range(2):
            for slot in range(6):
                fields[f][slot][pl.ds(36, 4), pl.ds(0, NY), :] = zero_side

    landed(0)
    depth = jnp.broadcast_to(extra[pl.ds(192, 8), pl.ds(9, 1)], (8, NZ))
    plane = jnp.where(lane.astype(jnp.float32) == depth, 0.5, 0.0)
    cell = jnp.broadcast_to(extra[pl.ds(192, 8), pl.ds(8, 1)], (8, NZ))
    turns = [(depth + m) - jnp.where(depth + m >= NZ, float(NZ), 0.0) for m in range(8)]

    def load_extra(j, carry):
        rows = pl.ds(pl.multiple_of(8 * j, 8), 8)
        records = [extra[pl.ds(pl.multiple_of(NY * h + 8 * j, 8), 8), :] for h in range(2)]
        for x in range(NX):
            placed = jnp.zeros((8, NZ), jnp.float32)
            for m in range(8):
                at = (m % 4) * NX + x
                value = jnp.broadcast_to(records[m // 4][:, at:at + 1], (8, NZ))
                placed = jnp.where(lane.astype(jnp.float32) == turns[m], value, placed)
            T[x, rows, :] = placed
            index = (place * NX + x) * (NY * NZ) + (row + 8 * j) * NZ + lane
            E[x, rows, :] = jnp.where(index.astype(jnp.float32) == cell, 0.5, 0.0)
        return carry

    lax.fori_loop(0, NY // 8, load_extra, 0)

    def clear(x, carry):
        image[x] = jnp.zeros((6, 16, NZ), jnp.float32)
        return carry

    lax.fori_loop(0, NX, clear, 0)

    def load_state(f, slot, source):
        def planes(picks):
            def tiles(j, carry):
                rows = pl.ds(pl.multiple_of(8 * j, 8), 8)
                for x in picks:
                    fields[f][slot][4 + x, rows, :] = source[pl.ds(8 * NX * j + x, 8, stride=NX), :]
                return carry
            lax.fori_loop(0, NY // 8, tiles, 0)

        planes([*range(4), *range(28, 32)])
        if slot == 1:
            send(f, 1, 0, 0)
            send(f, 1, 0, 1)
        planes(range(4, 28))

    first = blocks[xh * 8 + y * 2 + xl]

    def choose(first, row, b):
        half = (2 * row + b < first).astype(jnp.int32)
        step = 8 * half + 2 * row + b - first
        inside = (step >= 0).astype(jnp.int32) * (step < 6).astype(jnp.int32)
        return half + 2 * (1 - inside), step

    def packet(d, q):
        return raw_f.at[0, pl.ds(2 * CHUNK * (3 * q + d - 1), 2 * CHUNK), :]

    def total_of(k, q):
        return raw_f.at[1, pl.ds(CHUNK * (4 * q + k), CHUNK), :]

    def turn(d, q):
        return remote(packet(d, q), turned.at[q, d], isend.at[q, d - 1], irecv.at[q, d - 1],
                      device(xh, (y + d) % 4, core, z, xl))

    def pick_image(target, d, q):
        for b in range(2):
            half, step = choose(first, (y + d) % 4, b)
            value = image[pl.ds(NX // PARTS * q, NX // PARTS), jnp.clip(step, 0, 5), :, :] * 0.125
            target[pl.ds(CHUNK * b, CHUNK), :] = value.reshape(CHUNK, NZ)

    def send_image(q):
        for d in (2, 1, 3):
            pick_image(packet(d, q), d, q)
            turn(d, q).start()
        pick_image(turned.at[q, 0], 0, q)

    def mine(k):
        return (xh == k // 2) & (core == k % 2) & (xl == core)

    def line_copy(k):
        return remote(raw_a.at[0, pl.ds(4 * CHUNK * k, 4 * CHUNK), :], xfirst.at[xh * 2 + xl], csend.at[k],
                      crecv.at[xh * 2 + xl], device(k // 2, y, k % 2, z, core))

    def send_first():
        for k in range(4):
            for r in range(4):
                step = 8 * (k // 2) + 2 * r + k % 2 - first
                inside = (step >= 0).astype(jnp.int32) * (step < 6).astype(jnp.int32)
                value = image[pl.ds(0, NX // PARTS), jnp.clip(step, 0, 5), :, :] * 0.125
                kept = jnp.full((CHUNK, NZ), inside, jnp.int32) == 1
                raw_a[0, pl.ds(CHUNK * (4 * k + r), CHUNK), :] = jnp.where(kept, value.reshape(CHUNK, NZ), 0.0)

            @pl.when(jnp.logical_not(mine(k)))
            def _():
                line_copy(k).start()

            @pl.when(mine(k))
            def _():
                xfirst[xh * 2 + xl] = raw_a[0, pl.ds(4 * CHUNK * k, 4 * CHUNK), :]

    def column_copy(d):
        row = (y + d) % 4
        return remote(raw_a.at[1, pl.ds(pl.multiple_of(CHUNK * row, CHUNK), CHUNK), :], ysecond.at[d], dsend.at[d - 1],
                      drecv.at[d - 1], device(xh, row, core, z, xl))

    def across(f, slot, x, width):
        for h in range(0, width, 2):
            u = fields[f][slot][pl.ds(4 + x + h, 2), pl.ds(0, NY), :]
            high = u.astype(jnp.bfloat16)
            low = (u - high.astype(jnp.float32)).astype(jnp.bfloat16)
            high = jnp.concatenate([high[0], high[1]], axis=1)
            low = jnp.concatenate([low[0], low[1]], axis=1)
            rows = jnp.concatenate([high, low, band_y[...]], axis=1)
            columns = jnp.concatenate([band_z[...], high, low], axis=0)
            both = jnp.dot(rows, columns, preferred_element_type=jnp.float32)
            Z[f][x + h, pl.ds(0, NY), :] = both[:, :NZ]
            Z[f][x + h + 1, pl.ds(0, NY), :] = both[:, NZ:]

    def slot_of(n):
        return n + 1 if n < 5 else (n + 1) % 2

    def advance(f, n):
        cur, prev, new = fields[f][slot_of(n - 1)], fields[f][slot_of(n - 2)], fields[f][slot_of(n)]
        other = fields[1 - f][slot_of(9 - n)] if n > 4 else None
        wait(f, slot_of(n - 1), (n - 1) % 2)
        amp = jnp.broadcast_to(extra[pl.ds(192, 8), pl.ds(n - 1, 1)], (8, NZ))

        def planes(x, width):
            if f == 0 and n > 1:
                across(1, slot_of(n - 1), x, width)
            if f == 1 and n < 8:
                across(0, slot_of(n), x, width)
            for j in range(NY // 8):
                rows = pl.ds(8 * j, 8)
                wide = cur[pl.ds(x, width + 8), rows, :]
                u = wide[4:4 + width]
                acc = Z[f][pl.ds(x, width), rows, :]
                for k in range(1, 5):
                    acc = acc + WEIGHTS[k] * (wide[4 + k:4 + k + width] + wide[4 - k:4 - k + width])
                v = prev[pl.ds(4 + x, width), rows, :]
                if f == 0:
                    force = E[pl.ds(x, width), rows, :] * amp[None]
                else:
                    force = jnp.stack([pltpu.roll(T[x + h, rows, :], NZ - (8 - n), 1) * plane for h in range(width)])
                w = v + A[pl.ds(x, width), rows, :] * ((u - v) + (C[pl.ds(x, width), rows, :] * acc + force))
                new[pl.ds(4 + x, width), rows, :] = w
                if other is not None:
                    image[pl.ds(x, width), j // 2, pl.ds(8 * (j % 2), 8), :] += w * other[pl.ds(4 + x, width), rows, :]

        if f == 1 and n == 8:
            for i in range(PARTS):
                planes(WIDE * i, WIDE)
                if i == 0:
                    send_first()
                else:
                    send_image(i)
            return
        for x0, side in ((0, 0), (28, 1)):
            planes(x0, 4)
            if n < 8:
                send(f, slot_of(n), n % 2, side)

        def inner(i, carry):
            planes(4 + INNER * i, INNER)
            return carry

        lax.fori_loop(0, 24 // INNER, inner, 0)

    def first_across(f):
        def planes(i, carry):
            across(f, 1, WIDE * i, WIDE)
            return carry
        lax.fori_loop(0, NX // WIDE, planes, 0)

    landed(1)
    load_state(0, 1, raw_f.at[0])
    load_state(0, 0, raw_f.at[1])
    first_across(0)
    pick(ring.at[0], 0)
    for d in (1, 3, 2):
        round_trip(d).wait()


    def load_model(k, carry):
        j = first + k
        turn = (y - (j // 2) % 4 + 4) % 4
        parity = j % 2
        for h in range(2):
            rows = pl.ds(pl.multiple_of(16 * k + 8 * h, 8), 8)
            for x in range(NX):
                picked = pl.ds(8 * NX * h + x, 8, stride=NX)
                A[x, rows, :] = 2.0 / (1.0 + ring[turn, parity, 1, picked, :])
                C[x, rows, :] = ring[turn, parity, 0, picked, :] * (0.5 / SCALE)
        return carry

    lax.fori_loop(0, 6, load_model, 0)
    advance(0, 1)
    landed(2)
    load_state(1, 1, raw_a.at[0])
    first_across(1)
    landed(3)
    load_state(1, 0, raw_a.at[1])
    for n in range(1, 9):
        advance(1, n)
        if n < 8:
            advance(0, n + 1)

    def spread(k, q):
        return remote(total_of(k, q), lined.at[q, xh * 2 + xl], osend.at[q, k], orecv.at[q, xh * 2 + xl],
                      device(k // 2, y, k % 2, z, core))

    for k in range(4):
        @pl.when(jnp.logical_not((xh * 2 + xl == k) & (xl == core)))
        def _():
            remote(xfirst.at[k], xfirst.at[k], csend.at[0], crecv.at[k], device(k // 2, y, xl, z, k % 2)).wait_recv()
    raw_a[1, pl.ds(0, 4 * CHUNK), :] = (xfirst[0] + xfirst[1]) + (xfirst[2] + xfirst[3])
    for d in (2, 1, 3):
        column_copy(d).start()
    ysecond[0] = raw_a[1, pl.ds(pl.multiple_of(CHUNK * y, CHUNK), CHUNK), :]

    for q in range(1, PARTS):
        for d in (1, 3, 2):
            turn(d, q).wait_recv()
        for k in range(4):
            a, b = k // 2, k % 2
            total = jnp.zeros((CHUNK, NZ), jnp.float32)
            for d in range(4):
                half, step = choose(blocks[xh * 8 + ((y - d + 4) % 4) * 2 + xl], y, b)
                part = turned[q, d, pl.ds(CHUNK * b, CHUNK), :]
                total = total + jnp.where(jnp.full((CHUNK, NZ), half, jnp.int32) == a, part, 0.0)
            total_of(k, q)[...] = total

            @pl.when(jnp.logical_not(mine(k)))
            def _():
                spread(k, q).start()

            @pl.when(mine(k))
            def _():
                lined[q, xh * 2 + xl] = total_of(k, q)[...]

    for q in range(PARTS):
        if q == 0:
            for d in (1, 3, 2):
                column_copy(d).wait_recv()
            total = (ysecond[0] + ysecond[1]) + (ysecond[2] + ysecond[3])
        else:
            for k in range(4):
                @pl.when(jnp.logical_not((xh * 2 + xl == k) & (xl == core)))
                def _():
                    remote(lined.at[q, k], lined.at[q, k], osend.at[q, k], orecv.at[q, k],
                           device(k // 2, y, xl, z, k % 2)).wait_recv()
            total = (lined[q, 0] + lined[q, 1]) + (lined[q, 2] + lined[q, 3])
        for i in range(NX // PARTS):
            for h in range(2):
                out[pl.ds(8 * NX * h + NX // PARTS * q + i, 8, stride=NX), :] = total[16 * i + 8 * h:16 * i + 8 * h + 8]

    for d in (1, 3, 2):
        column_copy(d).wait_send()
    for k in range(4):
        @pl.when(jnp.logical_not(mine(k)))
        def _():
            line_copy(k).wait_send()
    for q in range(1, PARTS):
        for d in (1, 3, 2):
            turn(d, q).wait_send()
        for k in range(4):
            @pl.when(jnp.logical_not(mine(k)))
            def _():
                spread(k, q).wait_send()

    for copy in pair + cross:
        copy.wait_send()

    @pl.when(away)
    def _():
        for copy in inside + forward(0) + forward(1):
            copy.wait_send()
        for far, near in moves:
            far.wait_send()


def run_wave(blocks, wavelet, cell, depth, courant, damping, fwd, adj, records):
    vm = pl.BlockSpec(memory_space=pltpu.VMEM)
    scalars = pl.BlockSpec(memory_space=pltpu.SMEM)
    anywhere = pl.BlockSpec(memory_space=pl.ANY)
    dma = pltpu.SemaphoreType.DMA
    full = lambda: pltpu.VMEM((NX, PX, NZ), jnp.float32)
    flat = lambda *shape: pltpu.VMEM((*shape, NZ), jnp.float32)
    return pl.pallas_call(
        wave_kernel,
        out_shape=jax.ShapeDtypeStruct((512, NZ), jnp.float32),
        in_specs=[scalars] * 4 + [anywhere] * 4 + [vm] * 3,
        out_specs=vm,
        scratch_shapes=[
            *[flat(NX + 8, PY) for _ in range(12)],
            *[full() for _ in range(6)],
            flat(NX, 6, 16),
            flat(2, NY * NX),
            flat(2, NY * NX),
            flat(2 * NY + 8),
            flat(2 * NY + 8),
            flat(2, 2, 2, 512),
            flat(3, 2, 2, 512),
            flat(4, 2, 2, 512),
            flat(PARTS, 4, 2 * CHUNK),
            flat(PARTS, 4, CHUNK),
            dma((2, 2, 2)), dma((2, 2, 2)),
            dma((3, 2)), dma((2, 2, 2)), dma((2, 2)), dma((3,)), dma((3,)), dma((4,)), dma((4,)), dma((6,)),
            dma((PARTS, 3)), dma((PARTS, 3)), dma((PARTS, 4)), dma((PARTS, 4)),
            flat(4, 4 * CHUNK),
            flat(4, CHUNK),
            dma((4,)), dma((4,)), dma((3,)), dma((3,)),
        ],
        compiler_params=pltpu.CompilerParams(collective_id=1, has_side_effects=True, vmem_limit_bytes=61 << 20),
        name="wave_steps",
    )(blocks, wavelet, cell, depth, courant, damping, fwd, adj, records, *band_pair())


def body(courant, damping, aperture_block, source_cell, receiver_depth, wavelet, receiver_data,
         forward_state, adjoint_state):
    image = run_wave(aperture_block, wavelet, source_cell, receiver_depth, courant.reshape(512, NZ),
                     damping.reshape(512, NZ), forward_state[0].reshape(2, NY * NX, NZ),
                     adjoint_state[0].reshape(2, NY * NX, NZ), receiver_data[0].transpose(0, 2, 1))
    return image.reshape(16, NX, NZ)


def solution(mesh):
    placed = (
        P("shot", "tile", None),
        P("shot", "tile", None),
        P(),
        P("shot"),
        P("shot"),
        P("shot", None),
        P("shot", None, None, "tile"),
        P("shot", None, None, "tile", None),
        P("shot", None, None, "tile", None),
    )
    return jax.shard_map(
        body, mesh=mesh, in_specs=placed, out_specs=P("shot", "tile", None), check_vma=False
    )
```
